256 devices in a mesh: row: 128 (over z, x, y_lo, core), col: 2 (over y_hi).
Axes of the slice: x: 4, y: 4 (y_hi: 2, y_lo: 2; y = y_hi * 2 + y_lo), z: 8, core: 2. Of those that a mesh axis runs over, the one named last changes fastest.
Arguments:
- features: bfloat16 [65536, 128], P(('col', 'row')), may hold values from -6 to 6
- tile_values: bfloat16 [128, 2, 256, 128, 128], P('row', 'col'), may hold values from 0 to 3, as said below
- tile_rows: int32 [128, 2, 256], P('row', 'col'), may hold values from 0 to 3, as said below
- tile_cols: int32 [128, 2, 256], P('row', 'col'), may hold values from 0 to 1
- tile_counts: int32 [128, 2, 128], P('row', 'col'), may hold values from 0 to 2, as said below
- labels: int32 [65536], P(('col', 'row')), may hold values from 0 to 171
- w_self: bfloat16 [128, 256], replicated, may hold values from -0.5 to 0.5
- w_neigh: bfloat16 [128, 256], replicated, may hold values from -1 to 1
- bias: bfloat16 [256], replicated, may hold values from -3 to 3
- w_class: bfloat16 [256, 172], replicated, may hold values from -1 to 1
Outputs:
- hidden: bfloat16 [65536, 256], P(('col', 'row'))
- loss: float32 [], replicated
- grad_self: float32 [128, 256], replicated
- grad_neigh: float32 [128, 256], replicated
- grad_bias: float32 [256], replicated
- grad_class: float32 [256, 172], replicated
The draws below stay inside these ranges and needn't reach their ends.
Inputs may be any that keep to these rules, and one draw needn't show every extreme that they name: `tile_rows`: every slot index is below 4 for rows. `tile_counts`: at most 2 live slots for one source block, reached in every draw; slots at and beyond the count are ignored. `tile_values`: nonnegative edge weights, mostly zero.
All inputs are finite; a program needn't handle non-finite values.
Results may differ from the reference program's by a relative error of at most 0.012.
The reference program's roundings to bfloat16 on the way (of `mean`, `dlogits` and `dpre`) count: a program that leaves them out, or rounds other values in their place, can miss the bound.
Values may be sent and summed in bfloat16 or wider, within the bound.
No kernel may reach another device: no remote copies, remote signals or barrier semaphores. Data moves between devices by JAX's collectives and lax.ppermute only.
A program may use at most 128 MiB of HBM per device.

```python
import jax
import jax.numpy as jnp
from jax import lax

TILE = 128
F = 128
HID = 256
CLS = 172
NB_DEV = 2
KB = 2
NODES = 65536
N_ROW = 128
N_COL = 2


def draw_tile_values(key, part):
    key = jax.random.fold_in(key, 11)
    shape = (N_ROW, N_COL, N_ROW * KB, TILE, TILE)
    mask_key, level_key, lonely_key, pick_key = jax.random.split(key, 4)
    chance = min(0.5, 24.0 * NB_DEV / (N_ROW * TILE))
    keep = (jax.random.uniform(mask_key, shape, jnp.float32) < chance).astype(jnp.float32)
    lonely = jax.random.uniform(lonely_key, (N_ROW, TILE), jnp.float32) < 0.02
    picked = jax.random.randint(pick_key, (N_ROW, 1), 0, TILE)
    lonely = jnp.logical_or(lonely, jnp.arange(TILE, dtype=jnp.int32)[None, :] == picked)
    alive = 1.0 - lonely.astype(jnp.float32)
    alive = alive.reshape(N_ROW, 1, 1, TILE, 1)
    level = jax.random.uniform(level_key, shape, jnp.float32, 0.5, 2.0)
    return (keep * alive * level).astype(jnp.bfloat16)


def draw_tile_rows(key, part):
    key = jax.random.fold_in(key, 12)
    return jax.random.randint(key, (N_ROW, N_COL, N_ROW * KB), 0, 2 * NB_DEV).astype(jnp.int32)


def draw_tile_cols(key, part):
    key = jax.random.fold_in(key, 13)
    return jax.random.randint(key, (N_ROW, N_COL, N_ROW * KB), 0, NB_DEV).astype(jnp.int32)


def draw_tile_counts(key, part):
    key = jax.random.fold_in(key, 14)
    counts = jax.random.randint(key, (N_ROW, N_COL, N_ROW), 0, KB + 1).astype(jnp.int32)
    return counts.at[0, 0, 0].set(KB)


def place_ends(drawn, own_key, low, top_value):
    place = [jax.random.randint(jax.random.fold_in(own_key, axis), (), 0, length) for axis, length in enumerate(drawn.shape)]
    widest = drawn.shape.index(max(drawn.shape))
    neighbour = place[:widest] + [(place[widest] + 1) % drawn.shape[widest]] + place[widest + 1:]
    return drawn.at[tuple(place)].set(low).at[tuple(neighbour)].set(top_value)


def steps_of(rng, dims, cuts, smallest, high):
    def one(dim, parts):
        steps = jax.random.uniform(jax.random.fold_in(jax.random.fold_in(rng, 6), dim), (parts,), jnp.float32, smallest / len(cuts), high / len(cuts))
        return jnp.repeat(jnp.exp(steps), dims[dim] // parts).reshape((-1,) + (1,) * (len(dims) - dim - 1))

    gain = one(*cuts[0])
    for cut in cuts[1:]:
        gain = gain * one(*cut)
    return gain


def gaussian(stream_key, dims, spread, most, cuts=(), held_as=jnp.bfloat16):
    result = jax.random.normal(stream_key, dims, jnp.float32) * spread
    if len(cuts) > 0:
        result = steps_of(stream_key, dims, cuts, -0.22, 0.18) * result
    return jnp.clip(result, min=-most, max=most).astype(held_as)


def setup_inputs(seed: int = 0) -> dict:
    key_of = jax.random.split(jax.random.key(seed), 11)
    return {
        "features": gaussian(key_of[0], (NODES, F), 1.0, 6.0, ((0, 256),)),
        "tile_values": draw_tile_values(jax.random.fold_in(key_of[10], 71), 0),
        "tile_rows": draw_tile_rows(jax.random.fold_in(key_of[10], 71), 0),
        "tile_cols": draw_tile_cols(jax.random.fold_in(key_of[10], 71), 0),
        "tile_counts": draw_tile_counts(jax.random.fold_in(key_of[10], 71), 0),
        "labels": place_ends(jax.random.randint(key_of[5], (NODES,), 0, CLS), jax.random.fold_in(key_of[5], 1), 0, CLS - 1).astype(jnp.int32),
        "w_self": gaussian(key_of[6], (F, HID), F ** -0.5, 0.5),
        "w_neigh": gaussian(key_of[7], (F, HID), (F // 4) ** -0.5, 1.0),
        "bias": gaussian(key_of[8], (HID,), 0.5, 3.0),
        "w_class": gaussian(key_of[9], (HID, CLS), (HID // 8) ** -0.5, 1.0),
    }


def reference(features, tile_values, tile_rows, tile_cols, tile_counts, labels, w_self, w_neigh, bias, w_class):
    cycle = N_ROW
    block_nodes = NB_DEV * TILE
    total = cycle * N_COL * cycle * KB
    values = tile_values.reshape(total, TILE, TILE)
    rows = tile_rows.reshape(total)
    cols = tile_cols.reshape(total)

    def absorb(carry, index):
        summed, degree = carry
        r_idx = index // (N_COL * cycle * KB)
        c_idx = (index // (cycle * KB)) % N_COL
        source = (index // KB) % cycle
        k_idx = index % KB
        live = (k_idx < tile_counts[r_idx, c_idx, source]).astype(jnp.float32)
        t_row = rows[index]
        out_start = ((t_row // NB_DEV) * cycle + r_idx) * block_nodes + (t_row % NB_DEV) * TILE
        in_start = (c_idx * cycle + source) * block_nodes + cols[index] * TILE
        x_tile = lax.dynamic_slice_in_dim(features, in_start.astype(jnp.int32), TILE, 0)
        tile = values[index]
        product = jnp.dot(tile, x_tile, preferred_element_type=jnp.float32) * live
        sums_row = jnp.sum(tile.astype(jnp.float32), axis=1) * live
        old = lax.dynamic_slice_in_dim(summed, out_start.astype(jnp.int32), TILE, 0)
        summed = lax.dynamic_update_slice_in_dim(summed, old + product, out_start.astype(jnp.int32), 0)
        old_deg = lax.dynamic_slice_in_dim(degree, out_start.astype(jnp.int32), TILE, 0)
        degree = lax.dynamic_update_slice_in_dim(degree, old_deg + sums_row, out_start.astype(jnp.int32), 0)
        return (summed, degree), None

    start = (jnp.zeros((NODES, F), jnp.float32), jnp.zeros((NODES,), jnp.float32))
    (summed, degree), _ = lax.scan(absorb, start, jnp.arange(total, dtype=jnp.int32))
    mean = (summed / jnp.maximum(degree, 1.0)[:, None]).astype(jnp.bfloat16)
    pre = (jnp.dot(features, w_self, preferred_element_type=jnp.float32)
           + jnp.dot(mean, w_neigh, preferred_element_type=jnp.float32) + bias.astype(jnp.float32))
    hidden = jnp.maximum(pre, 0.0).astype(jnp.bfloat16)
    logits = jnp.dot(hidden, w_class, preferred_element_type=jnp.float32)
    logp = jax.nn.log_softmax(logits, axis=-1)
    onehot = (labels[:, None] == jnp.arange(CLS, dtype=jnp.int32)[None, :]).astype(jnp.float32)
    loss = -jnp.sum(onehot * logp) / NODES
    dlogits = ((jnp.exp(logp) - onehot) / NODES).astype(jnp.bfloat16)
    grad_class = jnp.dot(hidden.T, dlogits, preferred_element_type=jnp.float32)
    dhidden = jnp.dot(dlogits, w_class.T, preferred_element_type=jnp.float32)
    dpre = jnp.where(pre > 0, dhidden, 0.0).astype(jnp.bfloat16)
    grad_self = jnp.dot(features.T, dpre, preferred_element_type=jnp.float32)
    grad_neigh = jnp.dot(mean.T, dpre, preferred_element_type=jnp.float32)
    grad_bias = jnp.sum(dpre.astype(jnp.float32), axis=0)
    return hidden, loss, grad_self, grad_neigh, grad_bias, grad_class
```

```python
import functools

import jax
import jax.numpy as jnp
from jax import lax
from jax.experimental import pallas as pl
from jax.experimental.pallas import tpu as pltpu
from jax.sharding import Mesh, PartitionSpec as P

NZ, NX, NY, NC = 8, 4, 2, 2
ROW = ("z", "x", "yl", "co")
ALL = ("z", "x", "yl", "co", "yh")
TILE = 128
F = 128
HID = 256
CLS = 172
BLOCK = 256
NODES = 65536
CHIPS = NZ * NX * NY
PIECE = 8
DEAD = 8
VMEM = pl.BlockSpec(memory_space=pltpu.VMEM)
SMEM = pl.BlockSpec(memory_space=pltpu.SMEM)
ANY = pl.BlockSpec(memory_space=pl.ANY)


def index_of(z, x, yl, co):
    return ((z % NZ * NX + x % NX) * NY + yl % NY) * NC + co % NC


def move(value, target, cores=(0, 1)):
    pairs = []
    for z in range(NZ):
        for x in range(NX):
            for yl in range(NY):
                for co in cores:
                    pairs.append((index_of(z, x, yl, co), index_of(*target(z, x, yl, co))))
    return lax.ppermute(value, ROW, pairs)


def first(step):
    return lambda z, x, yl, co: (z, x + step, yl, co) if co == 0 else (z + step, x, yl, co)


def second(step):
    return lambda z, x, yl, co: (z + step, x, yl, co) if co == 0 else (z, x + step, yl, co)


def gather(own, core):
    other = move(own, lambda z, x, yl, co: (z, x, yl + 1, co))
    u = jnp.concatenate([own, other])
    a1, b1 = move(u, first(1)), move(u, first(-1))
    a2, b2 = move(a1, first(1)), move(b1, first(-1), (1,))
    here = jnp.concatenate([u, a1, b1, a2])
    p1, p2 = move(here, second(1)), move(here, second(-1))
    a3, b3 = move(a2, first(1), (1,)), move(b2, first(-1), (1,))
    c4 = move(a3, first(1), (1,))
    rest = jnp.concatenate([b2, a3, b3, c4])
    p3 = move(p1, second(1))
    p4 = move(jnp.where(core == 0, p2, rest), second(-1))
    p5 = move(jnp.where(core == 0, p3, rest), second(1))
    p6 = move(p4, second(-1))
    half = p5.shape[0] // 2
    far = jnp.concatenate([move(p5[:half], second(1), (0,)), move(p6[half:], second(-1), (0,))])
    return [here, p1, p2, p3, p4, p5, p6, jnp.where(core == 0, far, rest)]


def sources(z, x, yl, core):
    near, z_far = (0, 1, 3, 2), (6, 3, 5, 4)
    z_near = (0, 1, 7, 2)
    lists = []
    for piece in range(8):
        places = []
        for i in range(4):
            zo0, xo0 = (0, 1, 7, 2, 6, 3, 5, 4)[piece], near[i]
            zo1, xo1 = (z_near if piece < 4 else z_far)[i], (0, 1, 3, 2, 3, 1, 2, 0)[piece]
            zo = jnp.where(core == 0, zo0, zo1)
            xo = jnp.where(core == 0, xo0, xo1)
            for j in range(2):
                places.append(((z - zo) % NZ * NX + (x - xo) % NX) * NY + (yl + j) % NY)
        lists.append(jnp.stack(places).astype(jnp.int32))
    return lists


def degree_body(code_ref, tiles_ref, out_ref, acc):
    step = pl.program_id(0)
    count = tiles_ref.shape[0]

    @pl.when(step == 0)
    def _():
        acc[...] = jnp.zeros_like(acc)

    unit = jnp.ones((TILE, TILE), jnp.bfloat16)
    for k in range(count):
        start = pl.multiple_of((code_ref[step * count + k] // 2) * TILE, TILE)
        acc[pl.ds(start, TILE), :] += jnp.dot(
            tiles_ref[k], unit, preferred_element_type=jnp.float32
        )

    @pl.when(step == pl.num_programs(0) - 1)
    def _():
        out_ref[...] = acc[: out_ref.shape[0], :]


def degrees(codes, tiles):
    step = 16
    total = tiles.shape[0]
    return pl.pallas_call(
        degree_body,
        grid=(total // step,),
        in_specs=[SMEM, pl.BlockSpec((step, TILE, TILE), lambda i: (i, 0, 0))],
        out_specs=pl.BlockSpec((4 * TILE, TILE), lambda i: (0, 0)),
        out_shape=jax.ShapeDtypeStruct((4 * TILE, TILE), jnp.float32),
        scratch_shapes=[pltpu.VMEM((9 * TILE, TILE), jnp.float32)],
        cost_estimate=pl.CostEstimate(
            flops=2 * total * TILE**3, bytes_accessed=total * TILE * TILE * 2, transcendentals=0
        ),
    )(codes, tiles)


def piece_body(pieces, has_acc, *refs):
    core_ref, own_code, mate_code = refs[0], refs[1], refs[2]
    places = refs[3 : 3 + pieces]
    blocks = refs[3 + pieces : 3 + 2 * pieces]
    own_tiles, mate_tiles = refs[3 + 2 * pieces : 5 + 2 * pieces]
    rest = refs[5 + 2 * pieces :]
    acc_in = rest[0] if has_acc else None
    out_ref, acc, own_buf, mate_buf, sems = rest[1:] if has_acc else rest
    core = core_ref[0]
    copies = []
    for p in range(pieces):
        for i in range(PIECE):
            place = places[p][i]
            n = p * PIECE + i
            one = pltpu.make_async_copy(
                own_tiles.at[pl.ds((place * 2 + core) * 2, 2)], own_buf.at[pl.ds(2 * n, 2)], sems.at[2 * n]
            )
            two = pltpu.make_async_copy(
                mate_tiles.at[pl.ds(place * 2, 2)], mate_buf.at[pl.ds(2 * n, 2)], sems.at[2 * n + 1]
            )
            one.start()
            two.start()
            copies.append((one, two))
    if has_acc:
        acc[: 8 * TILE, :] = acc_in[...]
    else:
        acc[...] = jnp.zeros_like(acc)
    for p in range(pieces):
        for i in range(PIECE):
            place = places[p][i]
            n = p * PIECE + i
            copies[n][0].wait()
            copies[n][1].wait()
            for k in range(4):
                if k < 2:
                    code = own_code[(place * 2 + core) * 2 + k]
                    tile = own_buf[2 * n + k]
                else:
                    code = mate_code[place * 2 + k - 2]
                    tile = mate_buf[2 * n + k - 2]
                source = pl.multiple_of(i * BLOCK + (code % 2) * TILE, TILE)
                target = pl.multiple_of((code // 2) * TILE, TILE)
                acc[pl.ds(target, TILE), :] += jnp.dot(
                    tile, blocks[p][pl.ds(source, TILE), :], preferred_element_type=jnp.float32
                )
    out_ref[...] = acc[: 8 * TILE, :]


def absorb(core, own_code, mate_code, places, blocks, own_tiles, mate_tiles, acc):
    pieces = len(blocks)
    n = pieces * PIECE
    args = [core, own_code, mate_code, *places, *blocks, own_tiles, mate_tiles]
    specs = [SMEM] * (3 + pieces) + [VMEM] * pieces + [ANY, ANY]
    if acc is not None:
        args.append(acc)
        specs.append(VMEM)
    return pl.pallas_call(
        functools.partial(piece_body, pieces, acc is not None),
        in_specs=specs,
        out_specs=VMEM,
        out_shape=jax.ShapeDtypeStruct((8 * TILE, TILE), jnp.float32),
        scratch_shapes=[
            pltpu.VMEM((9 * TILE, TILE), jnp.float32),
            pltpu.VMEM((2 * n, TILE, TILE), jnp.bfloat16),
            pltpu.VMEM((2 * n, TILE, TILE), jnp.bfloat16),
            pltpu.SemaphoreType.DMA((2 * n,)),
        ],
        compiler_params=pltpu.CompilerParams(vmem_limit_bytes=24 * 2**20),
        cost_estimate=pl.CostEstimate(
            flops=8 * n * TILE**3, bytes_accessed=4 * n * TILE * TILE * 2 + 2**20, transcendentals=0
        ),
    )(*args)


def dense_body(
    feat, mine, theirs, deg_a, deg_b, labels, w_self, w_neigh, bias, w_class, hid_ref, grad_ref
):
    x = feat[...]
    degree = jnp.maximum(deg_a[...] + deg_b[...], 1.0)
    mean = ((mine[...] + theirs[...]) / degree).astype(jnp.bfloat16)
    pre = (
        jnp.dot(x, w_self[...], preferred_element_type=jnp.float32)
        + jnp.dot(mean, w_neigh[...], preferred_element_type=jnp.float32)
        + bias[...].astype(jnp.float32)
    )
    hidden = jnp.maximum(pre, 0.0).astype(jnp.bfloat16)
    hid_ref[...] = hidden
    logits = jnp.dot(hidden, w_class[...], preferred_element_type=jnp.float32)
    lane = lax.broadcasted_iota(jnp.int32, logits.shape, 1)
    valid = lane < CLS
    logits = jnp.where(valid, logits, -1e30)
    shifted = logits - jnp.max(logits, axis=1, keepdims=True)
    logp = shifted - jnp.log(jnp.sum(jnp.exp(shifted), axis=1, keepdims=True))
    hot = lane == labels[...]
    loss = -jnp.sum(jnp.where(hot, logp, 0.0))
    dlogits = ((jnp.exp(logp) - jnp.where(hot, 1.0, 0.0)) * (1.0 / NODES)).astype(jnp.bfloat16)
    rows = (((0,), (0,)), ((), ()))
    lanes = (((1,), (1,)), ((), ()))
    gclass = lax.dot_general(hidden, dlogits, rows, preferred_element_type=jnp.float32)
    dhidden = lax.dot_general(dlogits, w_class[...], lanes, preferred_element_type=jnp.float32)
    dpre = jnp.where(pre > 0, dhidden, 0.0).astype(jnp.bfloat16)
    ones = jnp.ones((BLOCK, HID), jnp.bfloat16)
    gbias = lax.dot_general(dpre, ones, rows, preferred_element_type=jnp.float32)
    high = loss.astype(jnp.bfloat16).astype(jnp.float32)
    low = (loss - high).astype(jnp.bfloat16).astype(jnp.float32)
    packed = jnp.where(lane == CLS, gbias, gclass)
    packed = jnp.where(lane == CLS + 1, high, packed)
    packed = jnp.where(lane == CLS + 2, low, packed)
    grad_ref[:HID, :] = packed.astype(grad_ref.dtype)
    grad_ref[HID : HID + F, :] = lax.dot_general(
        x, dpre, rows, preferred_element_type=jnp.float32
    ).astype(grad_ref.dtype)
    grad_ref[HID + F :, :] = lax.dot_general(
        mean, dpre, rows, preferred_element_type=jnp.float32
    ).astype(grad_ref.dtype)


def dense(*args):
    return pl.pallas_call(
        dense_body,
        in_specs=[VMEM] * len(args),
        out_specs=[VMEM, VMEM],
        out_shape=[
            jax.ShapeDtypeStruct((BLOCK, HID), jnp.bfloat16),
            jax.ShapeDtypeStruct((HID + 2 * F, HID), jnp.bfloat16),
        ],
        compiler_params=pltpu.CompilerParams(vmem_limit_bytes=24 * 2**20),
        cost_estimate=pl.CostEstimate(
            flops=2 * BLOCK * HID * 6 * HID, bytes_accessed=2**21, transcendentals=2 * BLOCK * HID
        ),
    )(*args)


def shards(
    features, tile_values, tile_rows, tile_cols, tile_counts, labels, w_self, w_neigh, bias, w_class
):
    z, x, yl, core, half = (lax.axis_index(a) for a in ALL)
    tiles = tile_values[0, 0]
    rows, cols, counts = tile_rows[0, 0], tile_cols[0, 0], tile_counts[0, 0]
    swap_core = lambda z, x, yl, co: (z, x, yl, co + 1)

    slot = jnp.arange(2, dtype=jnp.int32)[None, :]
    row_at = rows.reshape(-1, 2)
    target = (row_at // 2 != half).astype(jnp.int32) * 2 + row_at % 2
    code = target * 2 + cols.reshape(-1, 2)
    live = slot < counts[:, None]
    own_code = jnp.where(live, code, 2 * DEAD).reshape(-1)
    mate_send = jnp.where(live, code + 8, 2 * DEAD).reshape(CHIPS, 2, 2)
    mate_code = move(
        lax.dynamic_index_in_dim(mate_send, 1 - core, 1, keepdims=False).reshape(-1), swap_core
    )
    mate_tiles = move(
        lax.dynamic_index_in_dim(
            tiles.reshape(CHIPS, 2, 2, TILE, TILE), 1 - core, 1, keepdims=False
        ).reshape(2 * CHIPS, TILE, TILE),
        swap_core,
    )
    degree = degrees(own_code, tiles)
    other_degree = lax.ppermute(degree[BLOCK:], "yh", [(0, 1), (1, 0)])

    blocks = gather(features, core)
    places = sources(z, x, yl, core)
    core_at = core.reshape(1).astype(jnp.int32)
    acc = None
    for low, high in ((0, 3), (3, 5), (5, 8)):
        acc = absorb(
            core_at, own_code, mate_code, places[low:high], blocks[low:high], tiles, mate_tiles, acc
        )
    both = acc[: 2 * BLOCK] + move(acc[2 * BLOCK :], swap_core)
    theirs = lax.ppermute(both[BLOCK:], "yh", [(0, 1), (1, 0)])

    hidden, grads = dense(
        features,
        both[:BLOCK],
        theirs,
        degree[:BLOCK],
        other_degree,
        labels[:, None],
        w_self,
        w_neigh,
        bias[None, :],
        jnp.pad(w_class, ((0, 0), (0, HID - CLS))),
    )
    devices = NZ * NX * NY * NC * 2
    share = grads.shape[0] // devices
    parts = lax.all_to_all(grads, ALL, 0, 0, tiled=True).reshape(devices, share, HID)
    total = jnp.sum(parts.astype(jnp.float32), axis=0)
    whole = lax.all_to_all(jnp.tile(total, (devices, 1)), ALL, 0, 0, tiled=True)
    loss = (whole[0, CLS + 1] + whole[0, CLS + 2]) / NODES
    return (
        hidden,
        loss,
        whole[HID : HID + F],
        whole[HID + F :],
        whole[:HID, CLS],
        whole[:HID, :CLS],
    )


def solution(mesh):
    mesh = Mesh(mesh.devices.reshape(NZ, NX, NY, NC, 2), ALL)
    nodes = ("yh",) + ROW
    placed = (
        P(nodes, None),
        P(ROW, "yh", None, None, None),
        P(ROW, "yh", None),
        P(ROW, "yh", None),
        P(ROW, "yh", None),
        P(nodes),
        P(),
        P(),
        P(),
        P(),
    )
    return jax.shard_map(
        shards,
        mesh=mesh,
        in_specs=placed,
        out_specs=(P(nodes, None), P(), P(), P(), P(), P()),
        check_vma=False,
    )
```

```python
import functools

import jax
import jax.numpy as jnp
from jax import lax
from jax.experimental import pallas as pl
from jax.experimental.pallas import tpu as pltpu
from jax.sharding import Mesh, PartitionSpec as P

NZ, NX, NY, NC = 8, 4, 2, 2
ROW = ("z", "x", "yl", "co")
ALL = ("z", "x", "yl", "co", "yh")
TILE = 128
F = 128
HID = 256
CLS = 172
BLOCK = 256
NODES = 65536
DEAD = 8
LIMIT = 6 * 2**20
VMEM = pl.BlockSpec(memory_space=pltpu.VMEM)
ANY = pl.BlockSpec(memory_space=pl.ANY)
SMEM = pl.BlockSpec(memory_space=pltpu.SMEM)


def index_of(z, x, yl, co):
    return ((z % NZ * NX + x % NX) * NY + yl % NY) * NC + co % NC


def move(value, target, cores=(0, 1)):
    pairs = []
    for z in range(NZ):
        for x in range(NX):
            for yl in range(NY):
                for co in cores:
                    pairs.append((index_of(z, x, yl, co), index_of(*target(z, x, yl, co))))
    return lax.ppermute(value, ROW, pairs)


def first(step):
    return lambda z, x, yl, co: (z, x + step, yl, co) if co == 0 else (z + step, x, yl, co)


def second(step):
    return lambda z, x, yl, co: (z + step, x, yl, co) if co == 0 else (z, x + step, yl, co)


def sources(z, x, yl, core):
    x_steps, z_near, z_far = (0, 1, 3, 2), (0, 1, 7, 2), (6, 3, 5, 4)
    lists = []
    for piece in range(8):
        places = []
        for i in range(4):
            zo0, xo0 = (0, 1, 7, 2, 6, 3, 5, 4)[piece], x_steps[i]
            zo1, xo1 = (z_near if piece < 4 else z_far)[i], (0, 1, 3, 2, 0, 1, 3, 2)[piece]
            zo = jnp.where(core == 0, zo0, zo1)
            xo = jnp.where(core == 0, xo0, xo1)
            for j in range(2):
                places.append(((z - zo) % NZ * NX + (x - xo) % NX) * NY + (yl + j) % NY)
        lists.extend(places)
    return jnp.stack(lists).astype(jnp.int32)


def degree_body(code_ref, tiles_ref, out_ref, acc):
    acc[...] = jnp.zeros_like(acc)

    @pl.loop(0, tiles_ref.shape[0] // 16)
    def _(step):
        for k in range(16):
            n = step * 16 + k
            start = pl.multiple_of((code_ref[n] // 2) * TILE, TILE)
            acc[pl.ds(start, TILE), :] += tiles_ref[n].astype(jnp.float32)

    out_ref[...] = jnp.broadcast_to(
        jnp.sum(acc[: out_ref.shape[0], :], axis=1, keepdims=True), out_ref.shape
    )


def degrees(codes, tiles):
    total = tiles.shape[0]
    return pl.pallas_call(
        degree_body,
        in_specs=[SMEM, VMEM],
        out_specs=VMEM,
        out_shape=jax.ShapeDtypeStruct((4 * TILE, TILE), jnp.float32),
        scratch_shapes=[pltpu.VMEM((9 * TILE, TILE), jnp.float32)],
        compiler_params=pltpu.CompilerParams(vmem_limit_bytes=LIMIT),
        cost_estimate=pl.CostEstimate(
            flops=2 * total * TILE**2, bytes_accessed=total * TILE * TILE * 2, transcendentals=0
        ),
    )(codes, tiles)


def hold_body(core_ref, own_ref, mate_ref, out_ref, sems):
    core = core_ref[0]
    one = pltpu.make_async_copy(own_ref.at[:, core], out_ref.at[0], sems.at[0])
    two = pltpu.make_async_copy(mate_ref.at[:, core], out_ref.at[1], sems.at[1])
    one.start()
    two.start()
    one.wait()
    two.wait()


def hold(core, own_tiles, mate_tiles):
    chips = NZ * NX * NY
    shape = (chips, NC, 2, TILE, TILE)
    return pl.pallas_call(
        hold_body,
        in_specs=[SMEM, ANY, ANY],
        out_specs=VMEM,
        out_shape=pltpu.VMEM((2, chips, 2, TILE, TILE), jnp.bfloat16),
        scratch_shapes=[pltpu.SemaphoreType.DMA((2,))],
        compiler_params=pltpu.CompilerParams(vmem_limit_bytes=LIMIT),
        cost_estimate=pl.CostEstimate(flops=0, bytes_accessed=2**24, transcendentals=0),
    )(core, own_tiles.reshape(shape), mate_tiles.reshape(shape))


def piece_body(ranges, has_acc, split, *refs):
    core_ref, own_code, mate_code, places = refs[:4]
    blocks = refs[4 : 4 + len(ranges)]
    tiles = refs[4 + len(ranges)]
    rest = refs[5 + len(ranges) :]
    acc = rest[-1]
    core = core_ref[0]
    if has_acc:
        acc[: 8 * TILE, :] = rest[0][...]
        outs = rest[1:-1]
    else:
        acc[...] = jnp.zeros_like(acc)
        outs = rest[:-1]
    for block, (low, high) in zip(blocks, ranges):
        for i in range(high - low):
            place = places[low + i]
            for k in range(4):
                code = (own_code if k < 2 else mate_code)[(place * 2 + core) * 2 + k % 2]
                tile = tiles[k // 2, place, k % 2]
                source = pl.multiple_of(i * BLOCK + (code % 2) * TILE, TILE)
                target = pl.multiple_of((code // 2) * TILE, TILE)
                acc[pl.ds(target, TILE), :] += jnp.dot(
                    tile, block[pl.ds(source, TILE), :], preferred_element_type=jnp.float32
                )
    if split:
        outs[0][...] = acc[: 2 * TILE, :]
        outs[1][...] = acc[2 * TILE : 4 * TILE, :]
        outs[2][...] = acc[4 * TILE : 8 * TILE, :]
    else:
        outs[0][...] = acc[: 8 * TILE, :]


def absorb(tables, ranges, blocks, tiles, acc, split=False):
    n = sum(high - low for low, high in ranges)
    args = [*tables, *blocks, tiles]
    specs = [SMEM] * 4 + [VMEM] * (len(blocks) + 1)
    if acc is not None:
        args.append(acc)
        specs.append(VMEM)
    rows = (2, 2, 4) if split else (8,)
    out = pl.pallas_call(
        functools.partial(piece_body, ranges, acc is not None, split),
        in_specs=specs,
        out_specs=[VMEM] * len(rows),
        out_shape=[jax.ShapeDtypeStruct((r * TILE, TILE), jnp.float32) for r in rows],
        scratch_shapes=[pltpu.VMEM((9 * TILE, TILE), jnp.float32)],
        compiler_params=pltpu.CompilerParams(vmem_limit_bytes=LIMIT),
        cost_estimate=pl.CostEstimate(
            flops=8 * n * TILE**3, bytes_accessed=4 * n * TILE * TILE * 2 + 2**20, transcendentals=0
        ),
    )(*args)
    return out if split else out[0]


def aggregate(own, tiles, own_code, place, swap_core):
    z, x, yl, core, _ = place
    other = move(own, lambda z, x, yl, co: (z, x, yl + 1, co))
    mate_tiles = move(tiles, swap_core)
    mate_code = move(own_code, swap_core)
    mate_code = jnp.where(mate_code < 2 * DEAD, mate_code + DEAD, mate_code)
    u = jnp.concatenate([own, other])
    a1, b1 = move(u, first(1)), move(u, first(-1))
    a2, b2 = move(u, first(2)), move(u, first(-2), (1,))
    degree = degrees(own_code, tiles)
    here = jnp.concatenate([u, a1, b1, a2])
    here, degree = lax.optimization_barrier((here, degree))
    p1, p2 = move(here, second(1)), move(here, second(-1))
    tables = (core.reshape(1).astype(jnp.int32), own_code, mate_code, sources(z, x, yl, core))
    held = hold(tables[0], tiles, mate_tiles)
    acc = absorb(tables, [(0, 8)], [here], held, None)
    a3, b3 = move(a2, first(1), (1,)), move(b2, first(-1), (1,))
    c4 = move(a3, first(1), (1,))
    p1, p2, acc = lax.optimization_barrier((p1, p2, acc))
    p3, p4 = move(p1, second(1)), move(p2, second(-1), (0,))
    acc = absorb(tables, [(8, 16), (16, 24)], [p1, p2], held, acc)
    rest = jnp.concatenate([b2, a3, b3, c4])
    p3, p4, rest, acc = lax.optimization_barrier((p3, p4, rest, acc))
    p5 = move(jnp.where(core == 0, p3, rest), second(1))
    s4 = jnp.where(core == 0, p4, rest)
    p6 = move(s4, second(-1))
    acc = absorb(tables, [(24, 32), (32, 40)], [p3, s4], held, acc)
    p5, p6, acc = lax.optimization_barrier((p5, p6, acc))
    half = p5.shape[0] // 2
    p7, p8 = move(p5[:half], second(1)), move(p6[half:], second(-1))
    acc = absorb(tables, [(40, 48), (48, 56)], [p5, p6], held, acc)
    return degree, absorb(tables, [(56, 60), (60, 64)], [p7, p8], held, acc, True)


def dense_body(
    feat, mine, mates, theirs, deg_a, deg_b, labels, w_self, w_neigh, bias, w_class, hid_ref, grad_ref
):
    x = feat[...]
    degree = jnp.maximum(deg_a[...] + deg_b[...], 1.0)
    mean = ((mine[...] + mates[:BLOCK, :] + theirs[...]) / degree).astype(jnp.bfloat16)
    pre = (
        jnp.dot(x, w_self[...], preferred_element_type=jnp.float32)
        + jnp.dot(mean, w_neigh[...], preferred_element_type=jnp.float32)
        + bias[...].astype(jnp.float32)
    )
    hidden = jnp.maximum(pre, 0.0).astype(jnp.bfloat16)
    hid_ref[...] = hidden
    logits = jnp.dot(hidden, w_class[...], preferred_element_type=jnp.float32)
    lane = lax.broadcasted_iota(jnp.int32, logits.shape, 1)
    valid = lane < CLS
    logits = jnp.where(valid, logits, -1e30)
    shifted = logits - jnp.max(logits, axis=1, keepdims=True)
    logp = shifted - jnp.log(jnp.sum(jnp.exp(shifted), axis=1, keepdims=True))
    hot = lane == labels[...]
    loss = -jnp.sum(jnp.where(hot, logp, 0.0))
    dlogits = ((jnp.exp(logp) - jnp.where(hot, 1.0, 0.0)) * (1.0 / NODES)).astype(jnp.bfloat16)
    rows = (((0,), (0,)), ((), ()))
    lanes = (((1,), (1,)), ((), ()))
    gclass = lax.dot_general(hidden, dlogits, rows, preferred_element_type=jnp.float32)
    dhidden = lax.dot_general(dlogits, w_class[...], lanes, preferred_element_type=jnp.float32)
    dpre = jnp.where(pre > 0, dhidden, 0.0).astype(jnp.bfloat16)
    ones = jnp.ones((BLOCK, HID), jnp.bfloat16)
    gbias = lax.dot_general(dpre, ones, rows, preferred_element_type=jnp.float32)
    high = loss.astype(jnp.bfloat16).astype(jnp.float32)
    low = (loss - high).astype(jnp.bfloat16).astype(jnp.float32)
    packed = jnp.where(lane == CLS, gbias, gclass)
    packed = jnp.where(lane == CLS + 1, high, packed)
    packed = jnp.where(lane == CLS + 2, low, packed)
    grad_ref[:HID, :] = packed.astype(grad_ref.dtype)
    grad_ref[HID : HID + F, :] = lax.dot_general(
        x, dpre, rows, preferred_element_type=jnp.float32
    ).astype(grad_ref.dtype)
    grad_ref[HID + F :, :] = lax.dot_general(
        mean, dpre, rows, preferred_element_type=jnp.float32
    ).astype(grad_ref.dtype)


def dense(*args):
    return pl.pallas_call(
        dense_body,
        in_specs=[VMEM] * len(args),
        out_specs=[VMEM, VMEM],
        out_shape=[
            jax.ShapeDtypeStruct((BLOCK, HID), jnp.bfloat16),
            jax.ShapeDtypeStruct((HID + 2 * F, HID), jnp.bfloat16),
        ],
        compiler_params=pltpu.CompilerParams(vmem_limit_bytes=LIMIT),
        cost_estimate=pl.CostEstimate(
            flops=2 * BLOCK * HID * 6 * HID, bytes_accessed=2**21, transcendentals=2 * BLOCK * HID
        ),
    )(*args)


def finish_body(whole, loss_ref, self_ref, neigh_ref, bias_ref, class_ref):
    self_ref[...] = whole[HID : HID + F, :]
    neigh_ref[...] = whole[HID + F :, :]
    class_ref[...] = whole[:HID, :CLS]
    turned = jnp.transpose(whole[:HID, TILE:])
    bias_ref[...] = turned[CLS - TILE : CLS - TILE + 1, :]
    loss_ref[...] = (
        turned[CLS - TILE + 1 : CLS - TILE + 2, :TILE] + turned[CLS - TILE + 2 : CLS - TILE + 3, :TILE]
    ) * (1.0 / NODES)


def finish(whole):
    shapes = ((1, TILE), (F, HID), (F, HID), (1, HID), (HID, CLS))
    return pl.pallas_call(
        finish_body,
        in_specs=[VMEM],
        out_specs=[VMEM] * 5,
        out_shape=[jax.ShapeDtypeStruct(s, jnp.float32) for s in shapes],
    )(whole)


def shards(
    features, tile_values, tile_rows, tile_cols, tile_counts, labels, w_self, w_neigh, bias, w_class
):
    z, x, yl, core, half = (lax.axis_index(a) for a in ALL)
    tiles = tile_values[0, 0]
    rows, cols, counts = tile_rows[0, 0], tile_cols[0, 0], tile_counts[0, 0]
    swap_core = lambda z, x, yl, co: (z, x, yl, co + 1)

    slot = jnp.arange(2, dtype=jnp.int32)[None, :]
    row_at = rows.reshape(-1, 2)
    target = (row_at // 2 != half).astype(jnp.int32) * 2 + row_at % 2
    code = target * 2 + cols.reshape(-1, 2)
    own_code = jnp.where(slot < counts[:, None], code, 2 * DEAD).reshape(-1)
    degree, (mine, theirs, mates) = aggregate(
        features, tiles, own_code, (z, x, yl, core, half), swap_core
    )
    swap_half = [(0, 1), (1, 0)]
    other_degree = lax.ppermute(degree[BLOCK:], "yh", swap_half)
    mates = move(mates, swap_core)
    theirs = lax.ppermute(theirs + mates[BLOCK:], "yh", swap_half)

    hidden, grads = dense(
        features,
        mine,
        mates,
        theirs,
        degree[:BLOCK],
        other_degree,
        labels[:, None],
        w_self,
        w_neigh,
        bias[None, :],
        jnp.pad(w_class, ((0, 0), (0, HID - CLS))),
    )
    plane = ("x", "yl", "co", "yh")
    members = NX * NY * NC * 2
    share = grads.shape[0] // members
    parts = lax.all_to_all(grads, plane, 0, 0, tiled=True).reshape(members, share, HID)
    part = jnp.sum(parts.astype(jnp.float32), axis=0)
    parts = lax.all_to_all(jnp.tile(part, (NZ, 1)), "z", 0, 0, tiled=True)
    total = jnp.sum(parts.reshape(NZ, share, HID), axis=0)
    whole = lax.all_to_all(jnp.tile(total, (members, 1)), plane, 0, 0, tiled=True)
    loss, grad_self, grad_neigh, grad_bias, grad_class = finish(whole)
    return hidden, loss[0, 0], grad_self, grad_neigh, grad_bias[0], grad_class


def solution(mesh):
    mesh = Mesh(mesh.devices.reshape(NZ, NX, NY, NC, 2), ALL)
    nodes = ("yh",) + ROW
    placed = (
        P(nodes, None),
        P(ROW, "yh", None, None, None),
        P(ROW, "yh", None),
        P(ROW, "yh", None),
        P(ROW, "yh", None),
        P(nodes),
        P(),
        P(),
        P(),
        P(),
    )
    return jax.shard_map(
        shards,
        mesh=mesh,
        in_specs=placed,
        out_specs=(P(nodes, None), P(), P(), P(), P(), P()),
        check_vma=False,
    )
```

```python
import functools

import jax
import jax.numpy as jnp
from jax import lax
from jax.experimental import pallas as pl
from jax.experimental.pallas import tpu as pltpu
from jax.sharding import Mesh, PartitionSpec as P

NZ, NX, NY, NC = 8, 4, 2, 2
ROW = ("z", "x", "yl", "co")
ALL = ("z", "x", "yl", "co", "yh")
SWAP = [(0, 1), (1, 0)]
TILE = 128
F = 128
HID = 256
CLS = 172
BLOCK = 256
NODES = 65536
DEAD = 8
EXTRA = 176
LIMIT = 6 * 2**20
WIDE = 46 * 2**20
VMEM = pl.BlockSpec(memory_space=pltpu.VMEM)
ANY = pl.BlockSpec(memory_space=pl.ANY)
SMEM = pl.BlockSpec(memory_space=pltpu.SMEM)


def index_of(z, x, yl, co):
    return ((z % NZ * NX + x % NX) * NY + yl % NY) * NC + co % NC


def move(value, target, cores=(0, 1)):
    pairs = []
    for z in range(NZ):
        for x in range(NX):
            for yl in range(NY):
                for co in cores:
                    pairs.append((index_of(z, x, yl, co), index_of(*target(z, x, yl, co))))
    return lax.ppermute(value, ROW, pairs)


def first(step):
    return lambda z, x, yl, co: (z, x + step, yl, co) if co == 0 else (z + step, x, yl, co)


def second(step):
    return lambda z, x, yl, co: (z + step, x, yl, co) if co == 0 else (z, x + step, yl, co)


def sources(z, x, yl, core):
    x_steps, z_near, z_far = (0, 1, 3, 2), (0, 1, 7, 2), (6, 3, 5, 4)
    lists = []
    for piece in range(8):
        places = []
        for i in range(4):
            zo0, xo0 = (0, 1, 7, 2, 6, 3, 5, 4)[piece], x_steps[i]
            zo1, xo1 = (z_near if piece < 4 else z_far)[i], (0, 1, 3, 2, 0, 1, 3, 2)[piece]
            zo = jnp.where(core == 0, zo0, zo1)
            xo = jnp.where(core == 0, xo0, xo1)
            for j in range(2):
                places.append(((z - zo) % NZ * NX + (x - xo) % NX) * NY + (yl + j) % NY)
        lists.extend(places)
    return jnp.stack(lists).astype(jnp.int32)


def degree_body(code_ref, tiles_ref, out_ref, held, acc, sems):
    chunk = tiles_ref.shape[0] // sems.shape[0]

    def copy(step):
        part = pl.ds(step * chunk, chunk)
        return pltpu.make_async_copy(tiles_ref.at[part], held.at[part], sems.at[step])

    for step in range(sems.shape[0]):
        copy(step).start()
    acc[...] = jnp.zeros_like(acc)

    @pl.loop(0, sems.shape[0])
    def _(step):
        copy(step).wait()
        for i in range(chunk):
            n = step * chunk + i
            start = pl.multiple_of((code_ref[n] // 2) * TILE, TILE)
            acc[pl.ds(start, TILE), :] += held[n].astype(jnp.float32)

    out_ref[...] = jnp.broadcast_to(
        jnp.sum(acc[: out_ref.shape[0], :], axis=1, keepdims=True), out_ref.shape
    )


def degrees(codes, tiles):
    total = tiles.shape[0]
    return pl.pallas_call(
        degree_body,
        in_specs=[SMEM, ANY],
        out_specs=VMEM,
        out_shape=jax.ShapeDtypeStruct((4 * TILE, TILE), jnp.float32),
        scratch_shapes=[
            pltpu.VMEM(tiles.shape, tiles.dtype),
            pltpu.VMEM((9 * TILE, TILE), jnp.float32),
            pltpu.SemaphoreType.DMA((8,)),
        ],
        compiler_params=pltpu.CompilerParams(vmem_limit_bytes=WIDE),
        cost_estimate=pl.CostEstimate(
            flops=2 * total * TILE**2, bytes_accessed=total * TILE * TILE * 2, transcendentals=0
        ),
    )(codes, tiles)


def hold_body(core_ref, own_ref, mate_ref, out_ref, sems):
    core = core_ref[0]
    one = pltpu.make_async_copy(own_ref.at[:, core], out_ref.at[0], sems.at[0])
    two = pltpu.make_async_copy(mate_ref.at[:, core], out_ref.at[1], sems.at[1])
    one.start()
    two.start()
    one.wait()
    two.wait()


def hold(core, own_tiles, mate_tiles):
    chips = NZ * NX * NY
    shape = (chips, NC, 2, TILE, TILE)
    return pl.pallas_call(
        hold_body,
        in_specs=[SMEM, ANY, ANY],
        out_specs=VMEM,
        out_shape=pltpu.VMEM((2, chips, 2, TILE, TILE), jnp.bfloat16),
        scratch_shapes=[pltpu.SemaphoreType.DMA((2,))],
        compiler_params=pltpu.CompilerParams(vmem_limit_bytes=WIDE),
        cost_estimate=pl.CostEstimate(flops=0, bytes_accessed=2**24, transcendentals=0),
    )(core, own_tiles.reshape(shape), mate_tiles.reshape(shape))


def piece_body(ranges, has_acc, split, through, *refs):
    core_ref, own_code, mate_code, places = refs[:4]
    blocks = refs[4 : 4 + len(ranges)]
    tiles = refs[4 + len(ranges)]
    rest = refs[5 + len(ranges) :]
    acc = rest[-1]
    core = core_ref[0]
    if has_acc:
        acc[: 8 * TILE, :] = rest[0][...]
        outs = rest[1 + through : -1]
    else:
        acc[...] = jnp.zeros_like(acc)
        outs = rest[through:-1]
    for block, (low, high) in zip(blocks, ranges):
        for i in range(high - low):
            place = places[low + i]
            for k in range(4):
                code = (own_code if k < 2 else mate_code)[(place * 2 + core) * 2 + k % 2]
                tile = tiles[k // 2, place, k % 2]
                source = pl.multiple_of(i * BLOCK + (code % 2) * TILE, TILE)
                target = pl.multiple_of((code // 2) * TILE, TILE)
                acc[pl.ds(target, TILE), :] += jnp.dot(
                    tile, block[pl.ds(source, TILE), :], preferred_element_type=jnp.float32
                )
    if split:
        outs[0][...] = acc[: 2 * TILE, :]
        outs[1][...] = acc[2 * TILE : 4 * TILE, :]
        outs[2][...] = acc[4 * TILE : 8 * TILE, :]
    else:
        outs[0][...] = acc[: 8 * TILE, :]


def absorb(tables, ranges, blocks, tiles, acc, split=False, through=()):
    n = sum(high - low for low, high in ranges)
    args = [*tables, *blocks, tiles]
    specs = [SMEM] * 4 + [VMEM] * (len(blocks) + 1)
    if acc is not None:
        args.append(acc)
        specs.append(VMEM)
    rows = (2, 2, 4) if split else (8,)
    shapes = [jax.ShapeDtypeStruct((r * TILE, TILE), jnp.float32) for r in rows]
    outs = [VMEM] * len(rows)
    alias = {}
    for array in through:
        alias[len(args)] = len(outs)
        args.append(array)
        specs.append(ANY)
        shapes.append(jax.ShapeDtypeStruct(array.shape, array.dtype))
        outs.append(ANY)
    out = pl.pallas_call(
        functools.partial(piece_body, ranges, acc is not None, split, len(alias)),
        in_specs=specs,
        out_specs=outs,
        out_shape=shapes,
        input_output_aliases=alias,
        scratch_shapes=[pltpu.VMEM((9 * TILE, TILE), jnp.float32)],
        compiler_params=pltpu.CompilerParams(vmem_limit_bytes=LIMIT),
        cost_estimate=pl.CostEstimate(
            flops=8 * n * TILE**3, bytes_accessed=4 * n * TILE * TILE * 2 + 2**20, transcendentals=0
        ),
    )(*args)
    return out if len(outs) > 1 else out[0]


def assemble_body(count, *refs):
    out = refs[-1 - count]
    low = 0
    for ref in refs[: -1 - 2 * count]:
        out[low : low + ref.shape[0], :] = ref[...]
        low += ref.shape[0]


def assemble(parts, through):
    shape = (sum(p.shape[0] for p in parts), parts[0].shape[1])
    n = len(through)
    return pl.pallas_call(
        functools.partial(assemble_body, n),
        in_specs=[VMEM] * len(parts) + [ANY] * n,
        out_specs=[VMEM] + [ANY] * n,
        out_shape=[jax.ShapeDtypeStruct(shape, parts[0].dtype)]
        + [jax.ShapeDtypeStruct(t.shape, t.dtype) for t in through],
        input_output_aliases={len(parts) + i: 1 + i for i in range(n)},
        compiler_params=pltpu.CompilerParams(vmem_limit_bytes=LIMIT),
        cost_estimate=pl.CostEstimate(flops=0, bytes_accessed=2**20, transcendentals=0),
    )(*parts, *through)


def choose_body(core_ref, fore, back, *refs):
    out_fore, out_back = refs[-2:]

    @pl.when(core_ref[0] == 0)
    def _():
        out_fore[...] = fore[...]
        out_back[...] = back[...]

    @pl.when(core_ref[0] != 0)
    def _():
        low = 0
        for ref in refs[:-2]:
            out_fore[low : low + ref.shape[0], :] = ref[...]
            out_back[low : low + ref.shape[0], :] = ref[...]
            low += ref.shape[0]


def choose(core, fore, back, parts):
    return pl.pallas_call(
        choose_body,
        in_specs=[SMEM] + [VMEM] * (2 + len(parts)),
        out_specs=[VMEM] * 2,
        out_shape=[jax.ShapeDtypeStruct(fore.shape, fore.dtype)] * 2,
        compiler_params=pltpu.CompilerParams(vmem_limit_bytes=LIMIT),
        cost_estimate=pl.CostEstimate(flops=0, bytes_accessed=2**21, transcendentals=0),
    )(core, fore, back, *parts)


def aggregate(own, tiles, own_code, place, swap_core):
    z, x, yl, core, _ = place
    own_code, half_code = own_code
    other = move(own, lambda z, x, yl, co: (z, x, yl + 1, co))
    mate_tiles = move(tiles, swap_core)
    mate_code = move(half_code, swap_core)
    u = jnp.concatenate([own, other])
    a1, b1 = move(u, first(1)), move(u, first(-1))
    a2, b2 = move(u, first(2)), move(u, first(-2))
    degree = degrees(own_code, tiles)
    here, mate_tiles, degree, b2 = assemble([u, a1, b1, a2], [mate_tiles, degree, b2])
    p1, p2 = move(here, second(1)), move(here, second(-1))
    a3, b3 = move(a2, first(1)), move(b2, first(-1))
    core_at = core.reshape(1).astype(jnp.int32)
    tables = (core_at, own_code, mate_code, sources(z, x, yl, core))
    held = hold(core_at, tiles, mate_tiles)
    acc = absorb(tables, [(0, 8)], [here], held, None)
    p1, p2, acc = lax.optimization_barrier((p1, p2, acc))
    p3, p4 = move(p1, second(1)), move(p2, second(-1))
    c4 = move(a2, first(2))
    acc = absorb(tables, [(8, 16), (16, 24)], [p1, p2], held, acc)
    p3, p4, acc = lax.optimization_barrier((p3, p4, acc))
    s3, s4 = choose(core_at, p3, p4, [b2, a3, b3, c4])
    p5, p6 = move(s3, second(1)), move(s4, second(-1))
    other_degree = lax.ppermute(degree[BLOCK:], "yh", SWAP)
    acc = absorb(tables, [(24, 32), (32, 40)], [p3, s4], held, acc)
    p5, p6, acc, other_degree = lax.optimization_barrier((p5, p6, acc, other_degree))
    half = p5.shape[0] // 2
    p7, p8 = move(p5[:half], second(1)), move(p6[half:], second(-1))
    acc = absorb(tables, [(40, 48), (48, 56)], [p5, p6], held, acc)
    p7, p8, acc = lax.optimization_barrier((p7, p8, acc))
    sums = absorb(tables, [(56, 60), (60, 64)], [p7, p8], held, acc, split=True)
    return degree[:BLOCK], other_degree, sums


def put_loss(extra, loss):
    high = loss.astype(jnp.bfloat16).astype(jnp.float32)
    row = lax.broadcasted_iota(jnp.int32, extra.shape, 0)
    return jnp.where(row == 1, high, jnp.where(row == 2, loss - high, extra))


def dense_body(
    feat, mine, mates, theirs, deg_a, deg_b, labels, w_self, w_neigh, bias, w_class, hid_ref, grad_ref
):
    x = feat[...]
    degree = jnp.maximum(deg_a[...] + deg_b[...], 1.0)
    mean = ((mine[...] + mates[:BLOCK, :] + theirs[...]) / degree).astype(jnp.bfloat16)
    pre = (
        jnp.dot(x, w_self[...], preferred_element_type=jnp.float32)
        + jnp.dot(mean, w_neigh[...], preferred_element_type=jnp.float32)
        + bias[...].astype(jnp.float32)
    )
    hidden = jnp.maximum(pre, 0.0).astype(jnp.bfloat16)
    hid_ref[...] = hidden
    logits = lax.dot_general(
        hidden, w_class[...], (((1,), (1,)), ((), ())), preferred_element_type=jnp.float32
    )
    lane = lax.broadcasted_iota(jnp.int32, logits.shape, 1)
    logits = jnp.where(lane < CLS, logits, -1e30)
    shifted = logits - jnp.max(logits, axis=1, keepdims=True)
    logp = shifted - jnp.log(jnp.sum(jnp.exp(shifted), axis=1, keepdims=True))
    hot = lane == labels[...]
    loss = -jnp.sum(jnp.where(hot, logp, 0.0))
    dlogits = ((jnp.exp(logp) - jnp.where(hot, 1.0, 0.0)) * (1.0 / NODES)).astype(jnp.bfloat16)
    rows = (((0,), (0,)), ((), ()))
    dhidden = jnp.dot(dlogits, w_class[...], preferred_element_type=jnp.float32)
    dpre = jnp.where(pre > 0, dhidden, 0.0).astype(jnp.bfloat16)
    grad_ref[:HID, :] = lax.dot_general(
        dlogits, hidden, rows, preferred_element_type=jnp.float32
    ).astype(grad_ref.dtype)
    ones = jnp.ones((16, BLOCK), jnp.bfloat16)
    extra = jnp.dot(ones, dpre, preferred_element_type=jnp.float32)
    grad_ref[EXTRA : EXTRA + 16, :] = put_loss(extra, loss).astype(grad_ref.dtype)
    grad_ref[HID : HID + F, :] = lax.dot_general(
        x, dpre, rows, preferred_element_type=jnp.float32
    ).astype(grad_ref.dtype)
    grad_ref[HID + F :, :] = lax.dot_general(
        mean, dpre, rows, preferred_element_type=jnp.float32
    ).astype(grad_ref.dtype)


def dense(*args):
    return pl.pallas_call(
        dense_body,
        in_specs=[VMEM] * len(args),
        out_specs=[VMEM, VMEM],
        out_shape=[
            jax.ShapeDtypeStruct((BLOCK, HID), jnp.bfloat16),
            jax.ShapeDtypeStruct((HID + 2 * F, HID), jnp.bfloat16),
        ],
        compiler_params=pltpu.CompilerParams(vmem_limit_bytes=LIMIT),
        cost_estimate=pl.CostEstimate(
            flops=2 * BLOCK * HID * 6 * HID, bytes_accessed=2**21, transcendentals=2 * BLOCK * HID
        ),
    )(*args)


def fold_body(count, repeat, place_ref, parts, out_ref):
    share = parts.shape[0] // count
    total = parts[:share, :].astype(jnp.float32)
    for i in range(1, count):
        total += parts[i * share : (i + 1) * share, :].astype(jnp.float32)
    if out_ref.dtype == jnp.bfloat16:
        split = put_loss(total, total[1:2, :] + total[2:3, :])
        total = jnp.where(place_ref[0] == EXTRA // share, split, total)
    for i in range(repeat):
        out_ref[i * share : (i + 1) * share, :] = total.astype(out_ref.dtype)


def fold(place, parts, count, repeat, dtype):
    return pl.pallas_call(
        functools.partial(fold_body, count, repeat),
        in_specs=[SMEM, VMEM],
        out_specs=VMEM,
        out_shape=jax.ShapeDtypeStruct((parts.shape[0] // count * repeat, HID), dtype),
        compiler_params=pltpu.CompilerParams(vmem_limit_bytes=LIMIT),
    )(place, parts)


def finish_body(whole, loss_ref, self_ref, neigh_ref, bias_ref, class_ref):
    def rows(low, count):
        return whole[low : low + count, :].astype(jnp.float32)

    self_ref[...] = rows(HID, F)
    neigh_ref[...] = rows(HID + F, F)
    class_ref[...] = rows(0, EXTRA)[:CLS, :]
    extra = rows(EXTRA, 16)
    bias_ref[...] = extra[:1, :]
    loss_ref[...] = (extra[1:2, :TILE] + extra[2:3, :TILE]) * (1.0 / NODES)


def finish(whole):
    shapes = ((1, TILE), (F, HID), (F, HID), (1, HID), (CLS, HID))
    return pl.pallas_call(
        finish_body,
        in_specs=[VMEM],
        out_specs=[VMEM] * 5,
        out_shape=[jax.ShapeDtypeStruct(s, jnp.float32) for s in shapes],
        compiler_params=pltpu.CompilerParams(vmem_limit_bytes=LIMIT),
    )(whole)


def shards(
    features, tile_values, tile_rows, tile_cols, tile_counts, labels, w_self, w_neigh, bias, w_class
):
    z, x, yl, core, half = (lax.axis_index(a) for a in ALL)
    tiles = tile_values[0, 0]
    rows, cols, counts = tile_rows[0, 0], tile_cols[0, 0], tile_counts[0, 0]
    swap_core = lambda z, x, yl, co: (z, x, yl, co + 1)

    slot = jnp.arange(2, dtype=jnp.int32)[None, :]
    row_at = rows.reshape(-1, 2)
    target = (row_at // 2 != half).astype(jnp.int32) * 2 + row_at % 2
    code = target * 2 + cols.reshape(-1, 2)
    live = slot < counts[:, None]
    own_code = jnp.where(live, code, 2 * DEAD).reshape(-1)
    mate_code = jnp.where(live, code + DEAD, 2 * DEAD).reshape(-1)
    degree, other_degree, (mine, theirs, mates) = aggregate(
        features, tiles, (own_code, mate_code), (z, x, yl, core, half), swap_core
    )
    mates = move(mates, swap_core)
    theirs = lax.ppermute(theirs + mates[BLOCK:], "yh", SWAP)

    hidden, grads = dense(
        features,
        mine,
        mates,
        theirs,
        degree,
        other_degree,
        labels[:, None],
        w_self,
        w_neigh,
        bias[None, :],
        jnp.pad(w_class.T, ((0, HID - CLS), (0, 0))),
    )
    plane = ("x", "yl", "co", "yh")
    members = NX * NY * NC * 2
    member = lax.axis_index(plane).reshape(1).astype(jnp.int32)
    parts = lax.all_to_all(grads, plane, 0, 0, tiled=True)
    parts = lax.all_to_all(fold(member, parts, members, NZ, jnp.float32), "z", 0, 0, tiled=True)
    whole = lax.all_to_all(fold(member, parts, NZ, members, jnp.bfloat16), plane, 0, 0, tiled=True)
    loss, grad_self, grad_neigh, grad_bias, grad_class = finish(whole)
    return hidden, loss[0, 0], grad_self, grad_neigh, grad_bias[0], grad_class.T


def solution(mesh):
    mesh = Mesh(mesh.devices.reshape(NZ, NX, NY, NC, 2), ALL)
    nodes = ("yh",) + ROW
    placed = (
        P(nodes, None),
        P(ROW, "yh", None, None, None),
        P(ROW, "yh", None),
        P(ROW, "yh", None),
        P(ROW, "yh", None),
        P(nodes),
        P(),
        P(),
        P(),
        P(),
    )
    return jax.shard_map(
        shards,
        mesh=mesh,
        in_specs=placed,
        out_specs=(P(nodes, None), P(), P(), P(), P(), P()),
        check_vma=False,
    )
```

```python
import functools

import jax
import jax.numpy as jnp
from jax import lax
from jax.experimental import pallas as pl
from jax.experimental.pallas import tpu as pltpu
from jax.sharding import Mesh, PartitionSpec as P

NZ, NX, NY, NC = 8, 4, 2, 2
ROW = ("z", "x", "yl", "co")
ALL = ("z", "x", "yl", "co", "yh")
SWAP = [(0, 1), (1, 0)]
TILE = 128
F = 128
HID = 256
CLS = 172
BLOCK = 256
NODES = 65536
DEAD = 8
EXTRA = 176
LIMIT = 6 * 2**20
WIDE = 46 * 2**20
VMEM = pl.BlockSpec(memory_space=pltpu.VMEM)
ANY = pl.BlockSpec(memory_space=pl.ANY)
SMEM = pl.BlockSpec(memory_space=pltpu.SMEM)


def index_of(z, x, yl, co):
    return ((z % NZ * NX + x % NX) * NY + yl % NY) * NC + co % NC


def move(value, target, cores=(0, 1)):
    pairs = []
    for z in range(NZ):
        for x in range(NX):
            for yl in range(NY):
                for co in cores:
                    pairs.append((index_of(z, x, yl, co), index_of(*target(z, x, yl, co))))
    return lax.ppermute(value, ROW, pairs)


def first(step):
    return lambda z, x, yl, co: (z, x + step, yl, co) if co == 0 else (z + step, x, yl, co)


def second(step):
    return lambda z, x, yl, co: (z + step, x, yl, co) if co == 0 else (z, x + step, yl, co)


def sources(z, x, yl, core):
    x_steps, z_near, z_far = (0, 1, 3, 2), (0, 1, 7, 2), (6, 3, 5, 4)
    lists = []
    for piece in range(8):
        places = []
        for i in range(4):
            zo0, xo0 = (0, 1, 7, 2, 6, 3, 5, 4)[piece], x_steps[i]
            zo1, xo1 = (z_near if piece < 4 else z_far)[i], (0, 1, 3, 2, 0, 1, 3, 2)[piece]
            zo = jnp.where(core == 0, zo0, zo1)
            xo = jnp.where(core == 0, xo0, xo1)
            for j in range(2):
                places.append(((z - zo) % NZ * NX + (x - xo) % NX) * NY + (yl + j) % NY)
        lists.extend(places)
    return jnp.stack(lists).astype(jnp.int32)


def degree_body(code_ref, tiles_ref, out_ref, held, acc, sems):
    chunk = tiles_ref.shape[0] // sems.shape[0]

    def copy(step):
        part = pl.ds(step * chunk, chunk)
        return pltpu.make_async_copy(tiles_ref.at[part], held.at[part], sems.at[step])

    for step in range(sems.shape[0]):
        copy(step).start()
    acc[...] = jnp.zeros_like(acc)

    @pl.loop(0, sems.shape[0])
    def _(step):
        copy(step).wait()
        for i in range(chunk):
            n = step * chunk + i
            start = pl.multiple_of((code_ref[n] // 2) * TILE, TILE)
            acc[pl.ds(start, TILE), :] += held[n].astype(jnp.float32)

    out_ref[...] = jnp.broadcast_to(
        jnp.sum(acc[: out_ref.shape[0], :], axis=1, keepdims=True), out_ref.shape
    )


def degrees(codes, tiles):
    total = tiles.shape[0]
    return pl.pallas_call(
        degree_body,
        in_specs=[SMEM, ANY],
        out_specs=VMEM,
        out_shape=jax.ShapeDtypeStruct((4 * TILE, TILE), jnp.float32),
        scratch_shapes=[
            pltpu.VMEM(tiles.shape, tiles.dtype),
            pltpu.VMEM((9 * TILE, TILE), jnp.float32),
            pltpu.SemaphoreType.DMA((8,)),
        ],
        compiler_params=pltpu.CompilerParams(vmem_limit_bytes=WIDE),
        cost_estimate=pl.CostEstimate(
            flops=2 * total * TILE**2, bytes_accessed=total * TILE * TILE * 2, transcendentals=0
        ),
    )(codes, tiles)


def hold_body(core_ref, own_ref, mate_ref, after_ref, out_ref, sems):
    core = core_ref[0]
    one = pltpu.make_async_copy(own_ref.at[:, core], out_ref.at[0], sems.at[0])
    two = pltpu.make_async_copy(mate_ref.at[:, core], out_ref.at[1], sems.at[1])
    one.start()
    two.start()
    one.wait()
    two.wait()


def hold(core, own_tiles, mate_tiles, after):
    chips = NZ * NX * NY
    shape = (chips, NC, 2, TILE, TILE)
    return pl.pallas_call(
        hold_body,
        in_specs=[SMEM, ANY, ANY, ANY],
        out_specs=VMEM,
        out_shape=pltpu.VMEM((2, chips, 2, TILE, TILE), jnp.bfloat16),
        scratch_shapes=[pltpu.SemaphoreType.DMA((2,))],
        compiler_params=pltpu.CompilerParams(vmem_limit_bytes=WIDE),
        cost_estimate=pl.CostEstimate(flops=0, bytes_accessed=2**24, transcendentals=0),
    )(core, own_tiles.reshape(shape), mate_tiles.reshape(shape), after)


def piece_body(ranges, has_acc, split, through, *refs):
    core_ref, own_code, mate_code, places = refs[:4]
    blocks = refs[4 : 4 + len(ranges)]
    tiles = refs[4 + len(ranges)]
    rest = refs[5 + len(ranges) :]
    acc = rest[-1]
    core = core_ref[0]
    if has_acc:
        acc[: 8 * TILE, :] = rest[0][...]
        outs = rest[1 + through : -1]
    else:
        acc[...] = jnp.zeros_like(acc)
        outs = rest[through:-1]
    for block, (low, high) in zip(blocks, ranges):
        for i in range(high - low):
            place = places[low + i]
            for k in range(4):
                code = (own_code if k < 2 else mate_code)[(place * 2 + core) * 2 + k % 2]
                tile = tiles[k // 2, place, k % 2]
                source = pl.multiple_of(i * BLOCK + (code % 2) * TILE, TILE)
                target = pl.multiple_of((code // 2) * TILE, TILE)
                acc[pl.ds(target, TILE), :] += jnp.dot(
                    tile, block[pl.ds(source, TILE), :], preferred_element_type=jnp.float32
                )
    if split:
        outs[0][...] = acc[: 2 * TILE, :]
        outs[1][...] = acc[2 * TILE : 4 * TILE, :]
        outs[2][...] = acc[4 * TILE : 8 * TILE, :]
    else:
        outs[0][...] = acc[: 8 * TILE, :]


def absorb(tables, ranges, blocks, tiles, acc, split=False, through=()):
    n = sum(high - low for low, high in ranges)
    args = [*tables, *blocks, tiles]
    specs = [SMEM] * 4 + [VMEM] * (len(blocks) + 1)
    if acc is not None:
        args.append(acc)
        specs.append(VMEM)
    rows = (2, 2, 4) if split else (8,)
    shapes = [jax.ShapeDtypeStruct((r * TILE, TILE), jnp.float32) for r in rows]
    outs = [VMEM] * len(rows)
    alias = {}
    for array in through:
        alias[len(args)] = len(outs)
        args.append(array)
        specs.append(ANY)
        shapes.append(jax.ShapeDtypeStruct(array.shape, array.dtype))
        outs.append(ANY)
    out = pl.pallas_call(
        functools.partial(piece_body, ranges, acc is not None, split, len(alias)),
        in_specs=specs,
        out_specs=outs,
        out_shape=shapes,
        input_output_aliases=alias,
        scratch_shapes=[pltpu.VMEM((9 * TILE, TILE), jnp.float32)],
        compiler_params=pltpu.CompilerParams(vmem_limit_bytes=LIMIT),
        cost_estimate=pl.CostEstimate(
            flops=8 * n * TILE**3, bytes_accessed=4 * n * TILE * TILE * 2 + 2**20, transcendentals=0
        ),
    )(*args)
    return out if len(outs) > 1 else out[0]


def assemble_body(count, *refs):
    out = refs[-1 - count]
    low = 0
    for ref in refs[: -1 - 2 * count]:
        out[low : low + ref.shape[0], :] = ref[...]
        low += ref.shape[0]


def assemble(parts, through):
    shape = (sum(p.shape[0] for p in parts), parts[0].shape[1])
    n = len(through)
    return pl.pallas_call(
        functools.partial(assemble_body, n),
        in_specs=[VMEM] * len(parts) + [ANY] * n,
        out_specs=[VMEM] + [ANY] * n,
        out_shape=[jax.ShapeDtypeStruct(shape, parts[0].dtype)]
        + [jax.ShapeDtypeStruct(t.shape, t.dtype) for t in through],
        input_output_aliases={len(parts) + i: 1 + i for i in range(n)},
        compiler_params=pltpu.CompilerParams(vmem_limit_bytes=LIMIT),
        cost_estimate=pl.CostEstimate(flops=0, bytes_accessed=2**20, transcendentals=0),
    )(*parts, *through)


def choose_body(core_ref, fore, back, *refs):
    out_fore, out_back = refs[-2:]

    @pl.when(core_ref[0] == 0)
    def _():
        out_fore[...] = fore[...]
        out_back[...] = back[...]

    @pl.when(core_ref[0] != 0)
    def _():
        low = 0
        for ref in refs[:-2]:
            out_fore[low : low + ref.shape[0], :] = ref[...]
            out_back[low : low + ref.shape[0], :] = ref[...]
            low += ref.shape[0]


def choose(core, fore, back, parts):
    return pl.pallas_call(
        choose_body,
        in_specs=[SMEM] + [VMEM] * (2 + len(parts)),
        out_specs=[VMEM] * 2,
        out_shape=[jax.ShapeDtypeStruct(fore.shape, fore.dtype)] * 2,
        compiler_params=pltpu.CompilerParams(vmem_limit_bytes=LIMIT),
        cost_estimate=pl.CostEstimate(flops=0, bytes_accessed=2**21, transcendentals=0),
    )(core, fore, back, *parts)


def aggregate(own, tiles, own_code, place, swap_core):
    z, x, yl, core, _ = place
    own_code, half_code = own_code
    other = move(own, lambda z, x, yl, co: (z, x, yl + 1, co))
    mate_tiles = move(tiles, swap_core)
    mate_code = move(half_code, swap_core)
    u = jnp.concatenate([own, other])
    a1, b1 = move(u, first(1)), move(u, first(-1))
    a2, b2 = move(u, first(2)), move(u, first(-2))
    degree = degrees(own_code, tiles)
    here, mate_tiles, degree, b2 = assemble([u, a1, b1, a2], [mate_tiles, degree, b2])
    p1, p2 = move(here, second(1)), move(here, second(-1))
    a3, b3 = move(a2, first(1)), move(b2, first(-1))
    core_at = core.reshape(1).astype(jnp.int32)
    tables = (core_at, own_code, mate_code, sources(z, x, yl, core))
    p1, p2, a3, b3 = lax.optimization_barrier((p1, p2, a3, b3))
    p3, p4, c4 = move(p1, second(1)), move(p2, second(-1)), move(a3, first(1))
    held = hold(core_at, tiles, mate_tiles, p1)
    acc = absorb(tables, [(0, 8), (8, 16), (16, 24)], [here, p1, p2], held, None)
    p3, p4, c4, acc = lax.optimization_barrier((p3, p4, c4, acc))
    s3, s4 = choose(core_at, p3, p4, [b2, a3, b3, c4])
    half = s3.shape[0] // 2
    p5, p6 = move(s3, second(1)), move(s4, second(-1))
    p7, p8 = move(s3[:half], second(2)), move(s4[half:], second(-2))
    acc, degree = absorb(tables, [(24, 32), (32, 40)], [p3, s4], held, acc, through=[degree])
    other_degree = lax.ppermute(degree[BLOCK:], "yh", SWAP)
    p5, p6, acc = lax.optimization_barrier((p5, p6, acc))
    acc = absorb(tables, [(40, 48), (48, 56)], [p5, p6], held, acc)
    p7, p8, acc, other_degree = lax.optimization_barrier((p7, p8, acc, other_degree))
    sums = absorb(tables, [(56, 60), (60, 64)], [p7, p8], held, acc, split=True)
    return degree[:BLOCK], other_degree, sums


def put_loss(extra, loss):
    high = loss.astype(jnp.bfloat16).astype(jnp.float32)
    row = lax.broadcasted_iota(jnp.int32, extra.shape, 0)
    return jnp.where(row == 1, high, jnp.where(row == 2, loss - high, extra))


def dense_body(
    feat, mine, mates, theirs, deg_a, deg_b, labels, w_self, w_neigh, bias, w_class, hid_ref, grad_ref
):
    x = feat[...]
    degree = jnp.maximum(deg_a[...] + deg_b[...], 1.0)
    mean = ((mine[...] + mates[:BLOCK, :] + theirs[...]) / degree).astype(jnp.bfloat16)
    pre = (
        jnp.dot(x, w_self[...], preferred_element_type=jnp.float32)
        + jnp.dot(mean, w_neigh[...], preferred_element_type=jnp.float32)
        + bias[...].astype(jnp.float32)
    )
    hidden = jnp.maximum(pre, 0.0).astype(jnp.bfloat16)
    hid_ref[...] = hidden
    logits = lax.dot_general(
        hidden, w_class[...], (((1,), (1,)), ((), ())), preferred_element_type=jnp.float32
    )
    lane = lax.broadcasted_iota(jnp.int32, logits.shape, 1)
    logits = jnp.where(lane < CLS, logits, -1e30)
    shifted = logits - jnp.max(logits, axis=1, keepdims=True)
    logp = shifted - jnp.log(jnp.sum(jnp.exp(shifted), axis=1, keepdims=True))
    hot = lane == labels[...]
    loss = -jnp.sum(jnp.where(hot, logp, 0.0))
    dlogits = ((jnp.exp(logp) - jnp.where(hot, 1.0, 0.0)) * (1.0 / NODES)).astype(jnp.bfloat16)
    rows = (((0,), (0,)), ((), ()))
    dhidden = jnp.dot(dlogits, w_class[...], preferred_element_type=jnp.float32)
    dpre = jnp.where(pre > 0, dhidden, 0.0).astype(jnp.bfloat16)
    grad_ref[:HID, :] = lax.dot_general(
        dlogits, hidden, rows, preferred_element_type=jnp.float32
    ).astype(grad_ref.dtype)
    ones = jnp.ones((16, BLOCK), jnp.bfloat16)
    extra = jnp.dot(ones, dpre, preferred_element_type=jnp.float32)
    grad_ref[EXTRA : EXTRA + 16, :] = put_loss(extra, loss).astype(grad_ref.dtype)
    grad_ref[HID : HID + F, :] = lax.dot_general(
        x, dpre, rows, preferred_element_type=jnp.float32
    ).astype(grad_ref.dtype)
    grad_ref[HID + F :, :] = lax.dot_general(
        mean, dpre, rows, preferred_element_type=jnp.float32
    ).astype(grad_ref.dtype)


def dense(*args):
    return pl.pallas_call(
        dense_body,
        in_specs=[VMEM] * len(args),
        out_specs=[VMEM, VMEM],
        out_shape=[
            jax.ShapeDtypeStruct((BLOCK, HID), jnp.bfloat16),
            jax.ShapeDtypeStruct((HID + 2 * F, HID), jnp.bfloat16),
        ],
        compiler_params=pltpu.CompilerParams(vmem_limit_bytes=LIMIT),
        cost_estimate=pl.CostEstimate(
            flops=2 * BLOCK * HID * 6 * HID, bytes_accessed=2**21, transcendentals=2 * BLOCK * HID
        ),
    )(*args)


def fold_body(count, repeat, place_ref, parts, out_ref):
    share = parts.shape[0] // count
    total = parts[:share, :].astype(jnp.float32)
    for i in range(1, count):
        total += parts[i * share : (i + 1) * share, :].astype(jnp.float32)
    if out_ref.dtype == jnp.bfloat16:
        split = put_loss(total, total[1:2, :] + total[2:3, :])
        total = jnp.where(place_ref[0] == EXTRA // share, split, total)
    for i in range(repeat):
        out_ref[i * share : (i + 1) * share, :] = total.astype(out_ref.dtype)


def fold(place, parts, count, repeat, dtype):
    return pl.pallas_call(
        functools.partial(fold_body, count, repeat),
        in_specs=[SMEM, VMEM],
        out_specs=VMEM,
        out_shape=jax.ShapeDtypeStruct((parts.shape[0] // count * repeat, HID), dtype),
        compiler_params=pltpu.CompilerParams(vmem_limit_bytes=LIMIT),
    )(place, parts)


def finish_body(whole, loss_ref, self_ref, neigh_ref, bias_ref, class_ref):
    def rows(low, count):
        return whole[low : low + count, :].astype(jnp.float32)

    self_ref[...] = rows(HID, F)
    neigh_ref[...] = rows(HID + F, F)
    class_ref[...] = rows(0, EXTRA)[:CLS, :]
    extra = rows(EXTRA, 16)
    bias_ref[...] = extra[:1, :]
    loss_ref[...] = (extra[1:2, :TILE] + extra[2:3, :TILE]) * (1.0 / NODES)


def finish(whole):
    shapes = ((1, TILE), (F, HID), (F, HID), (1, HID), (CLS, HID))
    return pl.pallas_call(
        finish_body,
        in_specs=[VMEM],
        out_specs=[VMEM] * 5,
        out_shape=[jax.ShapeDtypeStruct(s, jnp.float32) for s in shapes],
        compiler_params=pltpu.CompilerParams(vmem_limit_bytes=LIMIT),
    )(whole)


def shards(
    features, tile_values, tile_rows, tile_cols, tile_counts, labels, w_self, w_neigh, bias, w_class
):
    z, x, yl, core, half = (lax.axis_index(a) for a in ALL)
    tiles = tile_values[0, 0]
    rows, cols, counts = tile_rows[0, 0], tile_cols[0, 0], tile_counts[0, 0]
    swap_core = lambda z, x, yl, co: (z, x, yl, co + 1)

    slot = jnp.arange(2, dtype=jnp.int32)[None, :]
    row_at = rows.reshape(-1, 2)
    target = (row_at // 2 != half).astype(jnp.int32) * 2 + row_at % 2
    code = target * 2 + cols.reshape(-1, 2)
    live = slot < counts[:, None]
    own_code = jnp.where(live, code, 2 * DEAD).reshape(-1)
    mate_code = jnp.where(live, code + DEAD, 2 * DEAD).reshape(-1)
    degree, other_degree, (mine, theirs, mates) = aggregate(
        features, tiles, (own_code, mate_code), (z, x, yl, core, half), swap_core
    )
    mates = move(mates, swap_core)
    theirs = lax.ppermute(theirs + mates[BLOCK:], "yh", SWAP)

    hidden, grads = dense(
        features,
        mine,
        mates,
        theirs,
        degree,
        other_degree,
        labels[:, None],
        w_self,
        w_neigh,
        bias[None, :],
        jnp.pad(w_class.T, ((0, HID - CLS), (0, 0))),
    )
    plane = ("x", "yl", "co", "yh")
    members = NX * NY * NC * 2
    member = lax.axis_index(plane).reshape(1).astype(jnp.int32)
    parts = lax.all_to_all(grads, plane, 0, 0, tiled=True)
    parts = lax.all_to_all(fold(member, parts, members, NZ, jnp.float32), "z", 0, 0, tiled=True)
    whole = lax.all_to_all(fold(member, parts, NZ, members, jnp.bfloat16), plane, 0, 0, tiled=True)
    loss, grad_self, grad_neigh, grad_bias, grad_class = finish(whole)
    return hidden, loss[0, 0], grad_self, grad_neigh, grad_bias[0], grad_class.T


def solution(mesh):
    mesh = Mesh(mesh.devices.reshape(NZ, NX, NY, NC, 2), ALL)
    nodes = ("yh",) + ROW
    placed = (
        P(nodes, None),
        P(ROW, "yh", None, None, None),
        P(ROW, "yh", None),
        P(ROW, "yh", None),
        P(ROW, "yh", None),
        P(nodes),
        P(),
        P(),
        P(),
        P(),
    )
    return jax.shard_map(
        shards,
        mesh=mesh,
        in_specs=placed,
        out_specs=(P(nodes, None), P(), P(), P(), P(), P()),
        check_vma=False,
    )
```

```python
import functools

import jax
import jax.numpy as jnp
from jax import lax
from jax.experimental import pallas as pl
from jax.experimental.pallas import tpu as pltpu
from jax.sharding import Mesh, PartitionSpec as P

NZ, NX, NY, NC = 8, 4, 2, 2
ROW = ("z", "x", "yl", "co")
ALL = ("z", "x", "yl", "co", "yh")
SWAP = [(0, 1), (1, 0)]
TILE = 128
F = 128
HID = 256
CLS = 172
BLOCK = 256
NODES = 65536
DEAD = 8
EXTRA = 176
LIMIT = 6 * 2**20
WIDE = 46 * 2**20
VMEM = pl.BlockSpec(memory_space=pltpu.VMEM)
ANY = pl.BlockSpec(memory_space=pl.ANY)
SMEM = pl.BlockSpec(memory_space=pltpu.SMEM)


def index_of(z, x, yl, co):
    return ((z % NZ * NX + x % NX) * NY + yl % NY) * NC + co % NC


def move(value, target, cores=(0, 1)):
    pairs = []
    for z in range(NZ):
        for x in range(NX):
            for yl in range(NY):
                for co in cores:
                    pairs.append((index_of(z, x, yl, co), index_of(*target(z, x, yl, co))))
    return lax.ppermute(value, ROW, pairs)


def first(step):
    return lambda z, x, yl, co: (z, x + step, yl, co) if co == 0 else (z + step, x, yl, co)


def second(step):
    return lambda z, x, yl, co: (z + step, x, yl, co) if co == 0 else (z, x + step, yl, co)


def sources(z, x, yl, core):
    x_steps, z_near, z_far = (0, 1, 3, 2), (0, 1, 7, 2), (6, 3, 5, 4)
    lists = []
    for piece in range(8):
        places = []
        for i in range(4):
            zo0, xo0 = (0, 1, 7, 2, 6, 3, 5, 4)[piece], x_steps[i]
            zo1, xo1 = (z_near if piece < 4 else z_far)[i], (0, 1, 3, 2, 0, 1, 3, 2)[piece]
            zo = jnp.where(core == 0, zo0, zo1)
            xo = jnp.where(core == 0, xo0, xo1)
            for j in range(2):
                places.append(((z - zo) % NZ * NX + (x - xo) % NX) * NY + (yl + j) % NY)
        lists.extend(places)
    return jnp.stack(lists).astype(jnp.int32)


def degree_body(code_ref, tiles_ref, out_ref, held, acc, sems):
    chunk = tiles_ref.shape[0] // sems.shape[0]

    def copy(step):
        part = pl.ds(step * chunk, chunk)
        return pltpu.make_async_copy(tiles_ref.at[part], held.at[part], sems.at[step])

    for step in range(sems.shape[0]):
        copy(step).start()
    acc[...] = jnp.zeros_like(acc)

    @pl.loop(0, sems.shape[0])
    def _(step):
        copy(step).wait()
        for i in range(chunk):
            n = step * chunk + i
            start = pl.multiple_of((code_ref[n] // 2) * TILE, TILE)
            acc[pl.ds(start, TILE), :] += held[n].astype(jnp.float32)

    out_ref[...] = jnp.broadcast_to(
        jnp.sum(acc[: out_ref.shape[0], :], axis=1, keepdims=True), out_ref.shape
    )


def degrees(codes, tiles):
    total = tiles.shape[0]
    return pl.pallas_call(
        degree_body,
        in_specs=[SMEM, ANY],
        out_specs=VMEM,
        out_shape=jax.ShapeDtypeStruct((4 * TILE, TILE), jnp.float32),
        scratch_shapes=[
            pltpu.VMEM(tiles.shape, tiles.dtype),
            pltpu.VMEM((9 * TILE, TILE), jnp.float32),
            pltpu.SemaphoreType.DMA((8,)),
        ],
        compiler_params=pltpu.CompilerParams(vmem_limit_bytes=WIDE),
        cost_estimate=pl.CostEstimate(
            flops=2 * total * TILE**2, bytes_accessed=total * TILE * TILE * 2, transcendentals=0
        ),
    )(codes, tiles)


def hold_body(core_ref, own_ref, mate_ref, out_ref, sems):
    core = core_ref[0]
    one = pltpu.make_async_copy(own_ref.at[:, core], out_ref.at[0], sems.at[0])
    two = pltpu.make_async_copy(mate_ref.at[:, core], out_ref.at[1], sems.at[1])
    one.start()
    two.start()
    one.wait()
    two.wait()


def hold(core, own_tiles, mate_tiles):
    chips = NZ * NX * NY
    shape = (chips, NC, 2, TILE, TILE)
    return pl.pallas_call(
        hold_body,
        in_specs=[SMEM, ANY, ANY],
        out_specs=VMEM,
        out_shape=pltpu.VMEM((2, chips, 2, TILE, TILE), jnp.bfloat16),
        scratch_shapes=[pltpu.SemaphoreType.DMA((2,))],
        compiler_params=pltpu.CompilerParams(vmem_limit_bytes=WIDE),
        cost_estimate=pl.CostEstimate(flops=0, bytes_accessed=2**24, transcendentals=0),
    )(core, own_tiles.reshape(shape), mate_tiles.reshape(shape))


def piece_body(ranges, has_acc, split, through, *refs):
    core_ref, own_code, mate_code, places = refs[:4]
    blocks = refs[4 : 4 + len(ranges)]
    tiles = refs[4 + len(ranges)]
    rest = refs[5 + len(ranges) :]
    acc = rest[-1]
    core = core_ref[0]
    if has_acc:
        acc[: 8 * TILE, :] = rest[0][...]
        outs = rest[1 + through : -1]
    else:
        acc[...] = jnp.zeros_like(acc)
        outs = rest[through:-1]
    for block, (low, high) in zip(blocks, ranges):
        for i in range(high - low):
            place = places[low + i]
            for k in range(4):
                code = (own_code if k < 2 else mate_code)[(place * 2 + core) * 2 + k % 2]
                tile = tiles[k // 2, place, k % 2]
                source = pl.multiple_of(i * BLOCK + (code % 2) * TILE, TILE)
                target = pl.multiple_of((code // 2) * TILE, TILE)
                acc[pl.ds(target, TILE), :] += jnp.dot(
                    tile, block[pl.ds(source, TILE), :], preferred_element_type=jnp.float32
                )
    if split:
        outs[0][...] = acc[: 2 * TILE, :]
        outs[1][...] = acc[2 * TILE : 4 * TILE, :]
        outs[2][...] = acc[4 * TILE : 8 * TILE, :]
    else:
        outs[0][...] = acc[: 8 * TILE, :]


def absorb(tables, ranges, blocks, tiles, acc, split=False, through=()):
    n = sum(high - low for low, high in ranges)
    args = [*tables, *blocks, tiles]
    specs = [SMEM] * 4 + [VMEM] * (len(blocks) + 1)
    if acc is not None:
        args.append(acc)
        specs.append(VMEM)
    rows = (2, 2, 4) if split else (8,)
    shapes = [jax.ShapeDtypeStruct((r * TILE, TILE), jnp.float32) for r in rows]
    outs = [VMEM] * len(rows)
    alias = {}
    for array in through:
        alias[len(args)] = len(outs)
        args.append(array)
        specs.append(ANY)
        shapes.append(jax.ShapeDtypeStruct(array.shape, array.dtype))
        outs.append(ANY)
    out = pl.pallas_call(
        functools.partial(piece_body, ranges, acc is not None, split, len(alias)),
        in_specs=specs,
        out_specs=outs,
        out_shape=shapes,
        input_output_aliases=alias,
        scratch_shapes=[pltpu.VMEM((9 * TILE, TILE), jnp.float32)],
        compiler_params=pltpu.CompilerParams(vmem_limit_bytes=LIMIT),
        cost_estimate=pl.CostEstimate(
            flops=8 * n * TILE**3, bytes_accessed=4 * n * TILE * TILE * 2 + 2**20, transcendentals=0
        ),
    )(*args)
    return out if len(outs) > 1 else out[0]


def assemble_body(count, *refs):
    out = refs[-1 - count]
    low = 0
    for ref in refs[: -1 - 2 * count]:
        out[low : low + ref.shape[0], :] = ref[...]
        low += ref.shape[0]


def assemble(parts, through):
    shape = (sum(p.shape[0] for p in parts), parts[0].shape[1])
    n = len(through)
    return pl.pallas_call(
        functools.partial(assemble_body, n),
        in_specs=[VMEM] * len(parts) + [ANY] * n,
        out_specs=[VMEM] + [ANY] * n,
        out_shape=[jax.ShapeDtypeStruct(shape, parts[0].dtype)]
        + [jax.ShapeDtypeStruct(t.shape, t.dtype) for t in through],
        input_output_aliases={len(parts) + i: 1 + i for i in range(n)},
        compiler_params=pltpu.CompilerParams(vmem_limit_bytes=LIMIT),
        cost_estimate=pl.CostEstimate(flops=0, bytes_accessed=2**20, transcendentals=0),
    )(*parts, *through)


def choose_body(core_ref, fore, back, *refs):
    out_fore, out_back = refs[-2:]

    @pl.when(core_ref[0] == 0)
    def _():
        out_fore[...] = fore[...]
        out_back[...] = back[...]

    @pl.when(core_ref[0] != 0)
    def _():
        low = 0
        for ref in refs[:-2]:
            out_fore[low : low + ref.shape[0], :] = ref[...]
            out_back[low : low + ref.shape[0], :] = ref[...]
            low += ref.shape[0]


def choose(core, fore, back, parts):
    return pl.pallas_call(
        choose_body,
        in_specs=[SMEM] + [VMEM] * (2 + len(parts)),
        out_specs=[VMEM] * 2,
        out_shape=[jax.ShapeDtypeStruct(fore.shape, fore.dtype)] * 2,
        compiler_params=pltpu.CompilerParams(vmem_limit_bytes=LIMIT),
        cost_estimate=pl.CostEstimate(flops=0, bytes_accessed=2**21, transcendentals=0),
    )(core, fore, back, *parts)


def aggregate(own, tiles, own_code, place, swap_core):
    z, x, yl, core, _ = place
    own_code, half_code = own_code
    other = move(own, lambda z, x, yl, co: (z, x, yl + 1, co))
    mate_tiles = move(tiles, swap_core)
    mate_code = move(half_code, swap_core)
    u = jnp.concatenate([own, other])
    a1, b1 = move(u, first(1)), move(u, first(-1))
    a2 = move(u, first(2))
    degree = degrees(own_code, tiles)
    here, mate_tiles, degree = assemble([u, a1, b1, a2], [mate_tiles, degree])
    p1, p2 = move(here, second(1)), move(here, second(-1))
    a3, b2 = move(a2, first(1)), move(b1, first(-1))
    core_at = core.reshape(1).astype(jnp.int32)
    tables = (core_at, own_code, mate_code, sources(z, x, yl, core))
    held = hold(core_at, tiles, mate_tiles)
    acc = absorb(tables, [(0, 8)], [here], held, None)
    p1, p2, a3, b2, acc = lax.optimization_barrier((p1, p2, a3, b2, acc))
    p3, p4 = move(p1, second(1)), move(p2, second(-1))
    c4, b3 = move(a3, first(1)), move(b2, first(-1))
    p3, p4, c4, b3, acc = lax.optimization_barrier((p3, p4, c4, b3, acc))
    s3, s4 = choose(core_at, p3, p4, [b2, a3, b3, c4])
    half = s3.shape[0] // 2
    p5, p6 = move(s3, second(1)), move(s4, second(-1))
    p7, p8 = move(s3[:half], second(2)), move(s4[half:], second(-2))
    acc, degree = absorb(
        tables, [(8, 16), (16, 24), (24, 32), (32, 40)], [p1, p2, p3, s4], held, acc, through=[degree]
    )
    other_degree = lax.ppermute(degree[BLOCK:], "yh", SWAP)
    p5, p6, acc = lax.optimization_barrier((p5, p6, acc))
    acc = absorb(tables, [(40, 48), (48, 56)], [p5, p6], held, acc)
    p7, p8, acc, other_degree = lax.optimization_barrier((p7, p8, acc, other_degree))
    sums = absorb(tables, [(56, 60), (60, 64)], [p7, p8], held, acc, split=True)
    return degree[:BLOCK], other_degree, sums


def put_loss(extra, loss):
    high = loss.astype(jnp.bfloat16).astype(jnp.float32)
    row = lax.broadcasted_iota(jnp.int32, extra.shape, 0)
    return jnp.where(row == 1, high, jnp.where(row == 2, loss - high, extra))


def dense_body(
    feat, mine, mates, theirs, deg_a, deg_b, labels, w_self, w_neigh, bias, w_class, hid_ref, grad_ref
):
    x = feat[...]
    degree = jnp.maximum(deg_a[...] + deg_b[...], 1.0)
    mean = ((mine[...] + mates[:BLOCK, :] + theirs[...]) / degree).astype(jnp.bfloat16)
    pre = (
        jnp.dot(x, w_self[...], preferred_element_type=jnp.float32)
        + jnp.dot(mean, w_neigh[...], preferred_element_type=jnp.float32)
        + bias[...].astype(jnp.float32)
    )
    hidden = jnp.maximum(pre, 0.0).astype(jnp.bfloat16)
    hid_ref[...] = hidden
    logits = lax.dot_general(
        hidden, w_class[...], (((1,), (1,)), ((), ())), preferred_element_type=jnp.float32
    )
    lane = lax.broadcasted_iota(jnp.int32, logits.shape, 1)
    logits = jnp.where(lane < CLS, logits, -1e30)
    shifted = logits - jnp.max(logits, axis=1, keepdims=True)
    logp = shifted - jnp.log(jnp.sum(jnp.exp(shifted), axis=1, keepdims=True))
    hot = lane == labels[...]
    loss = -jnp.sum(jnp.where(hot, logp, 0.0))
    dlogits = ((jnp.exp(logp) - jnp.where(hot, 1.0, 0.0)) * (1.0 / NODES)).astype(jnp.bfloat16)
    rows = (((0,), (0,)), ((), ()))
    dhidden = jnp.dot(dlogits, w_class[...], preferred_element_type=jnp.float32)
    dpre = jnp.where(pre > 0, dhidden, 0.0).astype(jnp.bfloat16)
    grad_ref[:HID, :] = lax.dot_general(
        dlogits, hidden, rows, preferred_element_type=jnp.float32
    ).astype(grad_ref.dtype)
    ones = jnp.ones((16, BLOCK), jnp.bfloat16)
    extra = jnp.dot(ones, dpre, preferred_element_type=jnp.float32)
    grad_ref[EXTRA : EXTRA + 16, :] = put_loss(extra, loss).astype(grad_ref.dtype)
    grad_ref[HID : HID + F, :] = lax.dot_general(
        x, dpre, rows, preferred_element_type=jnp.float32
    ).astype(grad_ref.dtype)
    grad_ref[HID + F :, :] = lax.dot_general(
        mean, dpre, rows, preferred_element_type=jnp.float32
    ).astype(grad_ref.dtype)


def dense(*args):
    return pl.pallas_call(
        dense_body,
        in_specs=[VMEM] * len(args),
        out_specs=[VMEM, VMEM],
        out_shape=[
            jax.ShapeDtypeStruct((BLOCK, HID), jnp.bfloat16),
            jax.ShapeDtypeStruct((HID + 2 * F, HID), jnp.bfloat16),
        ],
        compiler_params=pltpu.CompilerParams(vmem_limit_bytes=LIMIT),
        cost_estimate=pl.CostEstimate(
            flops=2 * BLOCK * HID * 6 * HID, bytes_accessed=2**21, transcendentals=2 * BLOCK * HID
        ),
    )(*args)


def fold_body(count, repeat, place_ref, parts, out_ref):
    share = parts.shape[0] // count
    total = parts[:share, :].astype(jnp.float32)
    for i in range(1, count):
        total += parts[i * share : (i + 1) * share, :].astype(jnp.float32)
    if out_ref.dtype == jnp.bfloat16:
        split = put_loss(total, total[1:2, :] + total[2:3, :])
        total = jnp.where(place_ref[0] == EXTRA // share, split, total)
    for i in range(repeat):
        out_ref[i * share : (i + 1) * share, :] = total.astype(out_ref.dtype)


def fold(place, parts, count, repeat, dtype):
    return pl.pallas_call(
        functools.partial(fold_body, count, repeat),
        in_specs=[SMEM, VMEM],
        out_specs=VMEM,
        out_shape=jax.ShapeDtypeStruct((parts.shape[0] // count * repeat, HID), dtype),
        compiler_params=pltpu.CompilerParams(vmem_limit_bytes=LIMIT),
    )(place, parts)


def finish_body(whole, loss_ref, self_ref, neigh_ref, bias_ref, class_ref):
    def rows(low, count):
        return whole[low : low + count, :].astype(jnp.float32)

    self_ref[...] = rows(HID, F)
    neigh_ref[...] = rows(HID + F, F)
    class_ref[...] = rows(0, EXTRA)[:CLS, :]
    extra = rows(EXTRA, 16)
    bias_ref[...] = extra[:1, :]
    loss_ref[...] = (extra[1:2, :TILE] + extra[2:3, :TILE]) * (1.0 / NODES)


def finish(whole):
    shapes = ((1, TILE), (F, HID), (F, HID), (1, HID), (CLS, HID))
    return pl.pallas_call(
        finish_body,
        in_specs=[VMEM],
        out_specs=[VMEM] * 5,
        out_shape=[jax.ShapeDtypeStruct(s, jnp.float32) for s in shapes],
        compiler_params=pltpu.CompilerParams(vmem_limit_bytes=LIMIT),
    )(whole)


def shards(
    features, tile_values, tile_rows, tile_cols, tile_counts, labels, w_self, w_neigh, bias, w_class
):
    z, x, yl, core, half = (lax.axis_index(a) for a in ALL)
    tiles = tile_values[0, 0]
    rows, cols, counts = tile_rows[0, 0], tile_cols[0, 0], tile_counts[0, 0]
    swap_core = lambda z, x, yl, co: (z, x, yl, co + 1)

    slot = jnp.arange(2, dtype=jnp.int32)[None, :]
    row_at = rows.reshape(-1, 2)
    target = (row_at // 2 != half).astype(jnp.int32) * 2 + row_at % 2
    code = target * 2 + cols.reshape(-1, 2)
    live = slot < counts[:, None]
    own_code = jnp.where(live, code, 2 * DEAD).reshape(-1)
    mate_code = jnp.where(live, code + DEAD, 2 * DEAD).reshape(-1)
    degree, other_degree, (mine, theirs, mates) = aggregate(
        features, tiles, (own_code, mate_code), (z, x, yl, core, half), swap_core
    )
    mates = move(mates, swap_core)
    theirs = lax.ppermute(theirs + mates[BLOCK:], "yh", SWAP)

    hidden, grads = dense(
        features,
        mine,
        mates,
        theirs,
        degree,
        other_degree,
        labels[:, None],
        w_self,
        w_neigh,
        bias[None, :],
        jnp.pad(w_class.T, ((0, HID - CLS), (0, 0))),
    )
    plane = ("x", "yl", "co", "yh")
    members = NX * NY * NC * 2
    member = lax.axis_index(plane).reshape(1).astype(jnp.int32)
    parts = lax.all_to_all(grads, plane, 0, 0, tiled=True)
    parts = lax.all_to_all(fold(member, parts, members, NZ, jnp.bfloat16), "z", 0, 0, tiled=True)
    whole = lax.all_to_all(fold(member, parts, NZ, members, jnp.bfloat16), plane, 0, 0, tiled=True)
    loss, grad_self, grad_neigh, grad_bias, grad_class = finish(whole)
    return hidden, loss[0, 0], grad_self, grad_neigh, grad_bias[0], grad_class.T


def solution(mesh):
    mesh = Mesh(mesh.devices.reshape(NZ, NX, NY, NC, 2), ALL)
    nodes = ("yh",) + ROW
    placed = (
        P(nodes, None),
        P(ROW, "yh", None, None, None),
        P(ROW, "yh", None),
        P(ROW, "yh", None),
        P(ROW, "yh", None),
        P(nodes),
        P(),
        P(),
        P(),
        P(),
    )
    return jax.shard_map(
        shards,
        mesh=mesh,
        in_specs=placed,
        out_specs=(P(nodes, None), P(), P(), P(), P(), P()),
        check_vma=False,
    )
```

```python
import functools

import jax
import jax.numpy as jnp
from jax import lax
from jax.experimental import pallas as pl
from jax.experimental.pallas import tpu as pltpu
from jax.sharding import Mesh, PartitionSpec as P

NZ, NX, NY, NC = 8, 4, 2, 2
ROW = ("z", "x", "yl", "co")
ALL = ("z", "x", "yl", "co", "yh")
SWAP = [(0, 1), (1, 0)]
TILE = 128
F = 128
HID = 256
CLS = 172
BLOCK = 256
NODES = 65536
DEAD = 8
EXTRA = 176
LIMIT = 6 * 2**20
WIDE = 46 * 2**20
VMEM = pl.BlockSpec(memory_space=pltpu.VMEM)
ANY = pl.BlockSpec(memory_space=pl.ANY)
SMEM = pl.BlockSpec(memory_space=pltpu.SMEM)


def index_of(z, x, yl, co):
    return ((z % NZ * NX + x % NX) * NY + yl % NY) * NC + co % NC


def move(value, target, cores=(0, 1)):
    pairs = []
    for z in range(NZ):
        for x in range(NX):
            for yl in range(NY):
                for co in cores:
                    pairs.append((index_of(z, x, yl, co), index_of(*target(z, x, yl, co))))
    return lax.ppermute(value, ROW, pairs)


def first(step):
    return lambda z, x, yl, co: (z, x + step, yl, co) if co == 0 else (z + step, x, yl, co)


def second(step):
    return lambda z, x, yl, co: (z + step, x, yl, co) if co == 0 else (z, x + step, yl, co)


def sources(z, x, yl, core):
    x_steps, z_near, z_far = (0, 1, 3, 2), (0, 1, 7, 2), (6, 3, 5, 4)
    lists = []
    for piece in range(8):
        places = []
        for i in range(4):
            zo0, xo0 = (0, 1, 7, 2, 6, 3, 5, 4)[piece], x_steps[i]
            zo1, xo1 = (z_near if piece < 4 else z_far)[i], (0, 1, 3, 2, 0, 1, 3, 2)[piece]
            zo = jnp.where(core == 0, zo0, zo1)
            xo = jnp.where(core == 0, xo0, xo1)
            for j in range(2):
                places.append(((z - zo) % NZ * NX + (x - xo) % NX) * NY + (yl + j) % NY)
        lists.extend(places)
    return jnp.stack(lists).astype(jnp.int32)


def degree_body(code_ref, tiles_ref, out_ref, held, acc, sems):
    chunk = tiles_ref.shape[0] // sems.shape[0]

    def copy(step):
        part = pl.ds(step * chunk, chunk)
        return pltpu.make_async_copy(tiles_ref.at[part], held.at[part], sems.at[step])

    for step in range(sems.shape[0]):
        copy(step).start()
    acc[...] = jnp.zeros_like(acc)

    @pl.loop(0, sems.shape[0])
    def _(step):
        copy(step).wait()
        for i in range(chunk):
            n = step * chunk + i
            start = pl.multiple_of((code_ref[n] // 2) * TILE, TILE)
            acc[pl.ds(start, TILE), :] += held[n].astype(jnp.float32)

    out_ref[...] = jnp.broadcast_to(
        jnp.sum(acc[: out_ref.shape[0], :], axis=1, keepdims=True), out_ref.shape
    )


def degrees(codes, tiles):
    total = tiles.shape[0]
    return pl.pallas_call(
        degree_body,
        in_specs=[SMEM, ANY],
        out_specs=VMEM,
        out_shape=jax.ShapeDtypeStruct((4 * TILE, TILE), jnp.float32),
        scratch_shapes=[
            pltpu.VMEM(tiles.shape, tiles.dtype),
            pltpu.VMEM((9 * TILE, TILE), jnp.float32),
            pltpu.SemaphoreType.DMA((8,)),
        ],
        compiler_params=pltpu.CompilerParams(vmem_limit_bytes=WIDE),
        cost_estimate=pl.CostEstimate(
            flops=2 * total * TILE**2, bytes_accessed=total * TILE * TILE * 2, transcendentals=0
        ),
    )(codes, tiles)


def hold_body(core_ref, own_ref, mate_ref, out_ref, sems):
    core = core_ref[0]
    one = pltpu.make_async_copy(own_ref.at[:, core], out_ref.at[0], sems.at[0])
    two = pltpu.make_async_copy(mate_ref.at[:, core], out_ref.at[1], sems.at[1])
    one.start()
    two.start()
    one.wait()
    two.wait()


def hold(core, own_tiles, mate_tiles):
    chips = NZ * NX * NY
    shape = (chips, NC, 2, TILE, TILE)
    return pl.pallas_call(
        hold_body,
        in_specs=[SMEM, ANY, ANY],
        out_specs=VMEM,
        out_shape=pltpu.VMEM((2, chips, 2, TILE, TILE), jnp.bfloat16),
        scratch_shapes=[pltpu.SemaphoreType.DMA((2,))],
        compiler_params=pltpu.CompilerParams(vmem_limit_bytes=WIDE),
        cost_estimate=pl.CostEstimate(flops=0, bytes_accessed=2**24, transcendentals=0),
    )(core, own_tiles.reshape(shape), mate_tiles.reshape(shape))


def piece_body(ranges, has_acc, split, through, *refs):
    core_ref, own_code, mate_code, places = refs[:4]
    blocks = refs[4 : 4 + len(ranges)]
    tiles = refs[4 + len(ranges)]
    rest = refs[5 + len(ranges) :]
    acc = rest[-1]
    core = core_ref[0]
    if has_acc:
        acc[: 8 * TILE, :] = rest[0][...]
        outs = rest[1 + through : -1]
    else:
        acc[...] = jnp.zeros_like(acc)
        outs = rest[through:-1]
    for block, (low, high) in zip(blocks, ranges):
        for i in range(high - low):
            place = places[low + i]
            for k in range(4):
                code = (own_code if k < 2 else mate_code)[(place * 2 + core) * 2 + k % 2]
                tile = tiles[k // 2, place, k % 2]
                source = pl.multiple_of(i * BLOCK + (code % 2) * TILE, TILE)
                target = pl.multiple_of((code // 2) * TILE, TILE)
                acc[pl.ds(target, TILE), :] += jnp.dot(
                    tile, block[pl.ds(source, TILE), :], preferred_element_type=jnp.float32
                )
    if split:
        outs[0][...] = acc[: 2 * TILE, :]
        outs[1][...] = acc[2 * TILE : 4 * TILE, :]
        outs[2][...] = acc[4 * TILE : 8 * TILE, :]
    else:
        outs[0][...] = acc[: 8 * TILE, :]


def absorb(tables, ranges, blocks, tiles, acc, split=False, through=()):
    n = sum(high - low for low, high in ranges)
    args = [*tables, *blocks, tiles]
    specs = [SMEM] * 4 + [VMEM] * (len(blocks) + 1)
    if acc is not None:
        args.append(acc)
        specs.append(VMEM)
    rows = (2, 2, 4) if split else (8,)
    shapes = [jax.ShapeDtypeStruct((r * TILE, TILE), jnp.float32) for r in rows]
    outs = [VMEM] * len(rows)
    alias = {}
    for array in through:
        alias[len(args)] = len(outs)
        args.append(array)
        specs.append(ANY)
        shapes.append(jax.ShapeDtypeStruct(array.shape, array.dtype))
        outs.append(ANY)
    out = pl.pallas_call(
        functools.partial(piece_body, ranges, acc is not None, split, len(alias)),
        in_specs=specs,
        out_specs=outs,
        out_shape=shapes,
        input_output_aliases=alias,
        scratch_shapes=[pltpu.VMEM((9 * TILE, TILE), jnp.float32)],
        compiler_params=pltpu.CompilerParams(vmem_limit_bytes=LIMIT),
        cost_estimate=pl.CostEstimate(
            flops=8 * n * TILE**3, bytes_accessed=4 * n * TILE * TILE * 2 + 2**20, transcendentals=0
        ),
    )(*args)
    return out if len(outs) > 1 else out[0]


def assemble_body(count, *refs):
    out = refs[-1 - count]
    low = 0
    for ref in refs[: -1 - 2 * count]:
        out[low : low + ref.shape[0], :] = ref[...]
        low += ref.shape[0]


def assemble(parts, through):
    shape = (sum(p.shape[0] for p in parts), parts[0].shape[1])
    n = len(through)
    return pl.pallas_call(
        functools.partial(assemble_body, n),
        in_specs=[VMEM] * len(parts) + [ANY] * n,
        out_specs=[VMEM] + [ANY] * n,
        out_shape=[jax.ShapeDtypeStruct(shape, parts[0].dtype)]
        + [jax.ShapeDtypeStruct(t.shape, t.dtype) for t in through],
        input_output_aliases={len(parts) + i: 1 + i for i in range(n)},
        compiler_params=pltpu.CompilerParams(vmem_limit_bytes=LIMIT),
        cost_estimate=pl.CostEstimate(flops=0, bytes_accessed=2**20, transcendentals=0),
    )(*parts, *through)


def choose_body(core_ref, fore, back, *refs):
    out_fore, out_back = refs[-2:]

    @pl.when(core_ref[0] == 0)
    def _():
        out_fore[...] = fore[...]
        out_back[...] = back[...]

    @pl.when(core_ref[0] != 0)
    def _():
        low = 0
        for ref in refs[:-2]:
            out_fore[low : low + ref.shape[0], :] = ref[...]
            out_back[low : low + ref.shape[0], :] = ref[...]
            low += ref.shape[0]


def choose(core, fore, back, parts):
    return pl.pallas_call(
        choose_body,
        in_specs=[SMEM] + [VMEM] * (2 + len(parts)),
        out_specs=[VMEM] * 2,
        out_shape=[jax.ShapeDtypeStruct(fore.shape, fore.dtype)] * 2,
        compiler_params=pltpu.CompilerParams(vmem_limit_bytes=LIMIT),
        cost_estimate=pl.CostEstimate(flops=0, bytes_accessed=2**21, transcendentals=0),
    )(core, fore, back, *parts)


def aggregate(own, tiles, own_code, place, swap_core):
    z, x, yl, core, _ = place
    own_code, half_code = own_code
    other = move(own, lambda z, x, yl, co: (z, x, yl + 1, co))
    mate_tiles = move(tiles, swap_core)
    mate_code = move(half_code, swap_core)
    u = jnp.concatenate([own, other])
    a1, b1 = move(u, first(1)), move(u, first(-1))
    a2 = move(u, first(2))
    degree = degrees(own_code, tiles)
    here, mate_tiles, degree = assemble([u, a1, b1, a2], [mate_tiles, degree])
    p1, p2 = move(here, second(1)), move(here, second(-1))
    a3, b2 = move(a2, first(1)), move(b1, first(-1))
    core_at = core.reshape(1).astype(jnp.int32)
    tables = (core_at, own_code, mate_code, sources(z, x, yl, core))
    held = hold(core_at, tiles, mate_tiles)
    acc = absorb(tables, [(0, 8)], [here], held, None)
    p1, p2, a3, b2, acc = lax.optimization_barrier((p1, p2, a3, b2, acc))
    p3, p4 = move(p1, second(1)), move(p2, second(-1))
    c4, b3 = move(a3, first(1)), move(b2, first(-1))
    p3, p4, c4, b3, acc = lax.optimization_barrier((p3, p4, c4, b3, acc))
    s3, s4 = choose(core_at, p3, p4, [b2, a3, b3, c4])
    half = s3.shape[0] // 2
    p5, p6 = move(s3, second(1)), move(s4, second(-1))
    p7, p8 = move(s3[:half], second(2)), move(s4[half:], second(-2))
    acc, degree = absorb(
        tables, [(8, 16), (16, 24), (24, 32), (32, 40)], [p1, p2, p3, s4], held, acc, through=[degree]
    )
    other_degree = lax.ppermute(degree[BLOCK:], "yh", SWAP)
    p5, p6, acc = lax.optimization_barrier((p5, p6, acc))
    acc = absorb(tables, [(40, 48), (48, 56)], [p5, p6], held, acc)
    p7, acc, other_degree = lax.optimization_barrier((p7, acc, other_degree))
    acc = absorb(tables, [(56, 60)], [p7], held, acc)
    p8, acc = lax.optimization_barrier((p8, acc))
    sums = absorb(tables, [(60, 64)], [p8], held, acc, split=True)
    return degree[:BLOCK], other_degree, sums


def put_loss(extra, loss):
    high = loss.astype(jnp.bfloat16).astype(jnp.float32)
    row = lax.broadcasted_iota(jnp.int32, extra.shape, 0)
    return jnp.where(row == 1, high, jnp.where(row == 2, loss - high, extra))


def dense_body(
    feat, mine, mates, theirs, deg_a, deg_b, labels, w_self, w_neigh, bias, w_class, hid_ref, grad_ref
):
    x = feat[...]
    degree = jnp.maximum(deg_a[...] + deg_b[...], 1.0)
    mean = ((mine[...] + mates[:BLOCK, :] + theirs[...].astype(jnp.float32)) / degree).astype(jnp.bfloat16)
    pre = (
        jnp.dot(x, w_self[...], preferred_element_type=jnp.float32)
        + jnp.dot(mean, w_neigh[...], preferred_element_type=jnp.float32)
        + bias[...].astype(jnp.float32)
    )
    hidden = jnp.maximum(pre, 0.0).astype(jnp.bfloat16)
    hid_ref[...] = hidden
    logits = lax.dot_general(
        hidden, w_class[...], (((1,), (1,)), ((), ())), preferred_element_type=jnp.float32
    )
    lane = lax.broadcasted_iota(jnp.int32, logits.shape, 1)
    logits = jnp.where(lane < CLS, logits, -1e30)
    shifted = logits - jnp.max(logits, axis=1, keepdims=True)
    logp = shifted - jnp.log(jnp.sum(jnp.exp(shifted), axis=1, keepdims=True))
    hot = lane == labels[...]
    loss = -jnp.sum(jnp.where(hot, logp, 0.0))
    dlogits = ((jnp.exp(logp) - jnp.where(hot, 1.0, 0.0)) * (1.0 / NODES)).astype(jnp.bfloat16)
    rows = (((0,), (0,)), ((), ()))
    dhidden = jnp.dot(dlogits, w_class[...], preferred_element_type=jnp.float32)
    dpre = jnp.where(pre > 0, dhidden, 0.0).astype(jnp.bfloat16)
    grad_ref[:HID, :] = lax.dot_general(
        dlogits, hidden, rows, preferred_element_type=jnp.float32
    ).astype(grad_ref.dtype)
    ones = jnp.ones((16, BLOCK), jnp.bfloat16)
    extra = jnp.dot(ones, dpre, preferred_element_type=jnp.float32)
    grad_ref[EXTRA : EXTRA + 16, :] = put_loss(extra, loss).astype(grad_ref.dtype)
    grad_ref[HID : HID + F, :] = lax.dot_general(
        x, dpre, rows, preferred_element_type=jnp.float32
    ).astype(grad_ref.dtype)
    grad_ref[HID + F :, :] = lax.dot_general(
        mean, dpre, rows, preferred_element_type=jnp.float32
    ).astype(grad_ref.dtype)


def dense(*args):
    return pl.pallas_call(
        dense_body,
        in_specs=[VMEM] * len(args),
        out_specs=[VMEM, VMEM],
        out_shape=[
            jax.ShapeDtypeStruct((BLOCK, HID), jnp.bfloat16),
            jax.ShapeDtypeStruct((HID + 2 * F, HID), jnp.bfloat16),
        ],
        compiler_params=pltpu.CompilerParams(vmem_limit_bytes=LIMIT),
        cost_estimate=pl.CostEstimate(
            flops=2 * BLOCK * HID * 6 * HID, bytes_accessed=2**21, transcendentals=2 * BLOCK * HID
        ),
    )(*args)


def fold_body(count, repeat, place_ref, parts, out_ref):
    share = parts.shape[0] // count
    total = parts[:share, :].astype(jnp.float32)
    for i in range(1, count):
        total += parts[i * share : (i + 1) * share, :].astype(jnp.float32)
    if out_ref.dtype == jnp.bfloat16:
        split = put_loss(total, total[1:2, :] + total[2:3, :])
        total = jnp.where(place_ref[0] == EXTRA // share, split, total)
    for i in range(repeat):
        out_ref[i * share : (i + 1) * share, :] = total.astype(out_ref.dtype)


def fold(place, parts, count, repeat, dtype):
    return pl.pallas_call(
        functools.partial(fold_body, count, repeat),
        in_specs=[SMEM, VMEM],
        out_specs=VMEM,
        out_shape=jax.ShapeDtypeStruct((parts.shape[0] // count * repeat, HID), dtype),
        compiler_params=pltpu.CompilerParams(vmem_limit_bytes=LIMIT),
    )(place, parts)


def finish_body(whole, loss_ref, self_ref, neigh_ref, bias_ref, class_ref):
    def rows(low, count):
        return whole[low : low + count, :].astype(jnp.float32)

    self_ref[...] = rows(HID, F)
    neigh_ref[...] = rows(HID + F, F)
    class_ref[...] = rows(0, EXTRA)[:CLS, :]
    extra = rows(EXTRA, 16)
    bias_ref[...] = extra[:1, :]
    loss_ref[...] = (extra[1:2, :TILE] + extra[2:3, :TILE]) * (1.0 / NODES)


def finish(whole):
    shapes = ((1, TILE), (F, HID), (F, HID), (1, HID), (CLS, HID))
    return pl.pallas_call(
        finish_body,
        in_specs=[VMEM],
        out_specs=[VMEM] * 5,
        out_shape=[jax.ShapeDtypeStruct(s, jnp.float32) for s in shapes],
        compiler_params=pltpu.CompilerParams(vmem_limit_bytes=LIMIT),
    )(whole)


def shards(
    features, tile_values, tile_rows, tile_cols, tile_counts, labels, w_self, w_neigh, bias, w_class
):
    z, x, yl, core, half = (lax.axis_index(a) for a in ALL)
    tiles = tile_values[0, 0]
    rows, cols, counts = tile_rows[0, 0], tile_cols[0, 0], tile_counts[0, 0]
    swap_core = lambda z, x, yl, co: (z, x, yl, co + 1)

    slot = jnp.arange(2, dtype=jnp.int32)[None, :]
    row_at = rows.reshape(-1, 2)
    target = (row_at // 2 != half).astype(jnp.int32) * 2 + row_at % 2
    code = target * 2 + cols.reshape(-1, 2)
    live = slot < counts[:, None]
    own_code = jnp.where(live, code, 2 * DEAD).reshape(-1)
    mate_code = jnp.where(live, code + DEAD, 2 * DEAD).reshape(-1)
    degree, other_degree, (mine, theirs, mates) = aggregate(
        features, tiles, (own_code, mate_code), (z, x, yl, core, half), swap_core
    )
    mates = move(mates, swap_core)
    theirs = lax.ppermute((theirs + mates[BLOCK:]).astype(jnp.bfloat16), "yh", SWAP)

    hidden, grads = dense(
        features,
        mine,
        mates,
        theirs,
        degree,
        other_degree,
        labels[:, None],
        w_self,
        w_neigh,
        bias[None, :],
        jnp.pad(w_class.T, ((0, HID - CLS), (0, 0))),
    )
    plane = ("x", "yl", "co", "yh")
    members = NX * NY * NC * 2
    member = lax.axis_index(plane).reshape(1).astype(jnp.int32)
    parts = lax.all_to_all(grads, plane, 0, 0, tiled=True)
    parts = lax.all_to_all(fold(member, parts, members, NZ, jnp.bfloat16), "z", 0, 0, tiled=True)
    whole = lax.all_to_all(fold(member, parts, NZ, members, jnp.bfloat16), plane, 0, 0, tiled=True)
    loss, grad_self, grad_neigh, grad_bias, grad_class = finish(whole)
    return hidden, loss[0, 0], grad_self, grad_neigh, grad_bias[0], grad_class.T


def solution(mesh):
    mesh = Mesh(mesh.devices.reshape(NZ, NX, NY, NC, 2), ALL)
    nodes = ("yh",) + ROW
    placed = (
        P(nodes, None),
        P(ROW, "yh", None, None, None),
        P(ROW, "yh", None),
        P(ROW, "yh", None),
        P(ROW, "yh", None),
        P(nodes),
        P(),
        P(),
        P(),
        P(),
    )
    return jax.shard_map(
        shards,
        mesh=mesh,
        in_specs=placed,
        out_specs=(P(nodes, None), P(), P(), P(), P(), P()),
        check_vma=False,
    )
```
